128 devices in a mesh: rows: 64 (over x, y_lo, z, core), frames: 2 (over y_hi).
Axes of the slice: x: 4, y: 4 (y_hi: 2, y_lo: 2; y = y_hi * 2 + y_lo), z: 4, core: 2. Of those that a mesh axis runs over, the one named last changes fastest.
Arguments:
- latents: bfloat16 [4, 128, 48, 640], P('frames', 'rows'), may hold values from -6 to 6
- previous: bfloat16 [4, 128, 48, 640], P('frames', 'rows'), may hold values from -6 to 6
- stale_normed: bfloat16 [4, 128, 48, 640], P('frames', 'rows'), may hold values from -6 to 6
- norm_gains: float32 [3, 640], replicated, may hold values from 0.1 to 1.9
- logit_scale: float32 [2, 10], replicated, may hold values from 1 to 10
- conv_weight: bfloat16 [9, 640, 640], replicated, may hold values from -0.078125 to 0.078125
- attn_weight: bfloat16 [640, 1920], replicated, may hold values from -0.25 to 0.25
- attn_out: bfloat16 [640, 640], replicated, may hold values from -0.25 to 0.25
- temporal_weight: bfloat16 [640, 1920], replicated, may hold values from -0.25 to 0.25
- temporal_out: bfloat16 [640, 640], replicated, may hold values from -0.25 to 0.25
- ff_in: bfloat16 [640, 5120], replicated, may hold values from -0.25 to 0.25
- ff_out: bfloat16 [2560, 640], replicated, may hold values from -0.125 to 0.125
Outputs:
- block_out: float32 [4, 128, 48, 640], P('frames', 'rows')
The draws below stay inside these ranges and needn't reach their ends.
All inputs are finite; a program needn't handle non-finite values.
Results may differ from the reference program's by a relative error of at most 0.019.
The reference program's roundings to bfloat16 on the way count: a program that leaves them out, or rounds other values in their place, can miss the bound.
Values may be sent and summed in bfloat16 or wider, within the bound.
A program may use at most 256 MiB of HBM per device.

```python
import math
import jax
import jax.numpy as jnp
from jax import lax

CHANNELS = 640
HEADS = 10
HEAD_DIM = 64
FF_HIDDEN = 2560
ROWS_DEV = 2
COLS = 48
ROWS = 128
FRAMES = 4
N_ROWS = 64


def draw_logit_scale(key, part):
    key = jax.random.fold_in(key, 7)
    base = jnp.exp(jax.random.uniform(key, (2, HEADS), jnp.float32, math.log(1.0), math.log(4.0)))
    return base


def steps_of(rng, extent, split, low, high):
    factor_of, own = 1.0, jax.random.fold_in(rng, 6)
    for axis_at, blocks in split:
        heights = jnp.exp(jax.random.uniform(jax.random.fold_in(own, axis_at), (blocks,), jnp.float32, low / len(split), high / len(split)))
        factor_of = factor_of * jnp.repeat(heights, extent[axis_at] // blocks).reshape([-1 if axis == axis_at else 1 for axis in range(len(extent))])
    return factor_of


def noise(rng, shape, deviation, bound, pieces=(), kind=jnp.bfloat16):
    factor_of = steps_of(rng, shape, pieces, -0.22, 0.18) if pieces else 1.0
    array = jax.random.normal(rng, shape, jnp.float32) * deviation * factor_of
    return jnp.minimum(jnp.maximum(array, -bound), bound).astype(kind)


def setup_inputs(seed: int = 0) -> dict:
    splits = jax.random.split(jax.random.key(seed), 13)
    latents = noise(splits[0], (FRAMES, ROWS, COLS, CHANNELS), 1.0, 6.0, ((0, 2), (1, 64)))
    previous = noise(splits[1], (FRAMES, ROWS, COLS, CHANNELS), 1.0, 6.0, ((0, 2), (1, 64)))
    stale_normed = noise(splits[2], (FRAMES, ROWS, COLS, CHANNELS), 1.0, 6.0, ((0, 2), (1, 64)))
    norm_gains = jnp.clip(1.0 + 0.18 * jax.random.normal(splits[3], (3, CHANNELS), jnp.float32), 0.1, 1.9)
    logit_scale = draw_logit_scale(jax.random.fold_in(splits[12], 71), 0)
    conv_weight = noise(splits[5], (9, CHANNELS, CHANNELS), (9 * CHANNELS) ** -0.5, 0.078125)
    attn_weight = noise(splits[6], (CHANNELS, 3 * CHANNELS), CHANNELS ** -0.5, 0.25)
    attn_out = noise(splits[7], (CHANNELS, CHANNELS), CHANNELS ** -0.5, 0.25)
    temporal_weight = noise(splits[8], (CHANNELS, 3 * CHANNELS), CHANNELS ** -0.5, 0.25)
    temporal_out = noise(splits[9], (CHANNELS, CHANNELS), CHANNELS ** -0.5, 0.25)
    ff_in = noise(splits[10], (CHANNELS, 2 * FF_HIDDEN), CHANNELS ** -0.5, 0.25)
    ff_out = noise(splits[11], (FF_HIDDEN, CHANNELS), FF_HIDDEN ** -0.5, 0.125)
    return {"latents": latents, "previous": previous, "stale_normed": stale_normed, "norm_gains": norm_gains, "logit_scale": logit_scale, "conv_weight": conv_weight, "attn_weight": attn_weight, "attn_out": attn_out, "temporal_weight": temporal_weight, "temporal_out": temporal_out, "ff_in": ff_in, "ff_out": ff_out}


NEG = -1e+30
EPS = 1e-05

def layer_norm(values, gain):
    centre = values - lax.optimization_barrier(jnp.mean(values, axis=-1, keepdims=True))
    spread = lax.optimization_barrier(jnp.mean(centre * centre, axis=-1, keepdims=True))
    return (centre * lax.rsqrt(spread + EPS) * gain).astype(jnp.bfloat16)

def activate(values):
    return jax.nn.silu(values.astype(jnp.float32)).astype(jnp.bfloat16)

def temporal_mix(queries, keys, values, scale):
    shape = queries.shape
    query_heads = queries.reshape(shape[0], -1, HEADS, HEAD_DIM).astype(jnp.float32)
    key_heads = keys.reshape(keys.shape[0], -1, HEADS, HEAD_DIM).astype(jnp.float32)
    value_heads = values.reshape(keys.shape[0], -1, HEADS, HEAD_DIM).astype(jnp.float32)
    scores = jnp.einsum('anhd,bnhd->nhab', query_heads, key_heads) * scale[None, :, None, None]
    peak = lax.optimization_barrier(jnp.max(scores, axis=-1, keepdims=True))
    weights = jnp.exp(scores - peak)
    total = lax.optimization_barrier(jnp.sum(weights, axis=-1))
    rounded = weights.astype(jnp.bfloat16).astype(jnp.float32)
    mixed = jnp.einsum('nhab,bnhd->anhd', rounded, value_heads)
    mixed = mixed / jnp.transpose(total, (2, 0, 1))[..., None]
    return mixed.astype(jnp.bfloat16).reshape(shape)

def reference(latents, previous, stale_normed, norm_gains, logit_scale, conv_weight, attn_weight, attn_out, temporal_weight, temporal_out, ff_in, ff_out):
    frames_all, rows_all, cols_all, width = latents.shape
    zero_row = jnp.zeros_like(latents[:, :1])
    latent_up = jnp.concatenate([zero_row, latents[:, :-1]], axis=1)
    prior_up = jnp.concatenate([zero_row, previous[:, :-1]], axis=1)
    latent_down = jnp.concatenate([latents[:, 1:], zero_row], axis=1)
    prior_down = jnp.concatenate([previous[:, 1:], zero_row], axis=1)
    row_index = jnp.arange(rows_all, dtype=jnp.int32)
    above = jnp.where((row_index % ROWS_DEV == 0)[None, :, None, None], prior_up, latent_up)
    below = jnp.where((row_index % ROWS_DEV == ROWS_DEV - 1)[None, :, None, None], prior_down, latent_down)
    fields = [activate(above), activate(latents), activate(below)]
    fields = [jnp.pad(item, ((0, 0), (0, 0), (1, 1), (0, 0))) for item in fields]
    conv_sum = jnp.zeros(latents.shape, jnp.float32)
    for row_step in range(3):
        for col_step in range(3):
            conv_sum = conv_sum + jnp.dot(fields[row_step][:, :, col_step:col_step + cols_all], conv_weight[row_step * 3 + col_step], preferred_element_type=jnp.float32)
    first = latents.astype(jnp.float32) + conv_sum
    normed = layer_norm(first, norm_gains[0])
    triple = jnp.dot(normed, attn_weight, preferred_element_type=jnp.float32).astype(jnp.bfloat16)
    stale_both = jnp.dot(stale_normed, attn_weight[:, width:], preferred_element_type=jnp.float32).astype(jnp.bfloat16)
    keys_old = stale_both[..., :width].reshape(frames_all, rows_all * cols_all, HEADS, HEAD_DIM).astype(jnp.float32)
    values_old = stale_both[..., width:].reshape(frames_all, rows_all * cols_all, HEADS, HEAD_DIM).astype(jnp.float32)
    scale = logit_scale[0] / math.sqrt(HEAD_DIM)
    key_rows = jnp.repeat(jnp.arange(rows_all, dtype=jnp.int32), cols_all)

    def patch(index):
        start = (index * ROWS_DEV).astype(jnp.int32)

        def take(tensor):
            piece = lax.dynamic_slice_in_dim(tensor, start, ROWS_DEV, 1)
            return piece.reshape(frames_all, ROWS_DEV * cols_all, HEADS, HEAD_DIM).astype(jnp.float32)
        query_heads = take(triple[..., :width])
        keys_new = take(triple[..., width:2 * width])
        values_new = take(triple[..., 2 * width:])
        keep = (key_rows < start) | (key_rows >= start + ROWS_DEV)
        score_old = jnp.einsum('fqhd,fkhd->fhqk', query_heads, keys_old) * scale[None, :, None, None]
        score_old = jnp.where(keep, score_old, NEG)
        score_new = jnp.einsum('fqhd,fkhd->fhqk', query_heads, keys_new) * scale[None, :, None, None]
        peak = jnp.maximum(lax.optimization_barrier(jnp.max(score_old, axis=-1)), lax.optimization_barrier(jnp.max(score_new, axis=-1)))
        weight_old = jnp.where(keep, jnp.exp(score_old - peak[..., None]), 0.0)
        weight_new = jnp.exp(score_new - peak[..., None])
        total = lax.optimization_barrier(jnp.sum(weight_old, axis=-1)) + lax.optimization_barrier(jnp.sum(weight_new, axis=-1))
        accum = jnp.einsum('fhqk,fkhd->fhqd', weight_old.astype(jnp.bfloat16).astype(jnp.float32), values_old)
        accum = accum + jnp.einsum('fhqk,fkhd->fhqd', weight_new.astype(jnp.bfloat16).astype(jnp.float32), values_new)
        mixed = accum / total[..., None]
        mixed = jnp.transpose(mixed, (0, 2, 1, 3)).reshape(frames_all, ROWS_DEV, cols_all, width)
        return mixed.astype(jnp.bfloat16)
    patches = lax.map(patch, jnp.arange(N_ROWS, dtype=jnp.int32))
    spatial_mix = jnp.moveaxis(patches, 0, 1).reshape(frames_all, rows_all, cols_all, width)
    second = first + jnp.dot(spatial_mix, attn_out, preferred_element_type=jnp.float32)
    normed_two = layer_norm(second, norm_gains[1])
    triple_two = jnp.dot(normed_two, temporal_weight, preferred_element_type=jnp.float32).astype(jnp.bfloat16)
    time_scale = logit_scale[1] / math.sqrt(HEAD_DIM)
    mixed_time = temporal_mix(triple_two[..., :width], triple_two[..., width:2 * width], triple_two[..., 2 * width:], time_scale)
    third = second + jnp.dot(mixed_time, temporal_out, preferred_element_type=jnp.float32)
    normed_three = layer_norm(third, norm_gains[2])
    both = jnp.dot(normed_three, ff_in, preferred_element_type=jnp.float32)
    half = ff_out.shape[0]
    ff_hidden = (both[..., :half] * jax.nn.gelu(both[..., half:], approximate=False)).astype(jnp.bfloat16)
    return third + jnp.dot(ff_hidden, ff_out, preferred_element_type=jnp.float32)
```

```python
import functools
import math

import jax
import jax.numpy as jnp
from jax import lax
from jax.experimental import pallas as pl
from jax.experimental.pallas import tpu as pltpu
from jax.sharding import PartitionSpec as P

HEADS = 10
HEAD_DIM = 64
NEG = -1e30
EPS = 1e-05
F32 = jnp.float32
BF16 = jnp.bfloat16
MESH = pl.DeviceIdType.MESH
NT = (((1,), (1,)), ((), ()))
PATCH = 96
QUERIES = 384
PAIRS = 3
HALF = 384


def extended(cells, sides, width):
    for axis, dim in sides:
        count = lax.axis_size(axis)
        ends = count - 1
        head = lax.slice_in_dim(cells, 0, width, axis=dim)
        tail = lax.slice_in_dim(cells, cells.shape[dim] - width, cells.shape[dim], axis=dim)
        cells = jnp.concatenate(
            [
                lax.ppermute(tail, axis, [(i, (i + 1) % count) for i in range(ends)]),
                cells,
                lax.ppermute(head, axis, [((i + 1) % count, i) for i in range(ends)]),
            ],
            axis=dim,
        )
    return cells


def layer_norm(values, gain):
    centre = values - jnp.mean(values, axis=-1, keepdims=True)
    spread = jnp.mean(centre * centre, axis=-1, keepdims=True)
    return (centre * lax.rsqrt(spread + EPS) * gain).astype(BF16)


def temporal_mix(queries, keys, values, scale):
    shape = queries.shape
    query_heads = queries.reshape(shape[0], -1, HEADS, HEAD_DIM)
    key_heads = keys.reshape(keys.shape[0], -1, HEADS, HEAD_DIM)
    value_heads = values.reshape(keys.shape[0], -1, HEADS, HEAD_DIM)
    scores = (
        jnp.einsum("anhd,bnhd->nhab", query_heads, key_heads, preferred_element_type=F32)
        * scale[None, :, None, None]
    )
    peak = jnp.max(scores, axis=-1, keepdims=True)
    weights = jnp.exp(scores - peak)
    total = jnp.sum(weights, axis=-1)
    mixed = jnp.einsum(
        "nhab,bnhd->anhd", weights.astype(BF16), value_heads, preferred_element_type=F32
    )
    mixed = mixed / jnp.transpose(total, (2, 0, 1))[..., None]
    return mixed.astype(BF16).reshape(shape)


def spatial_kernel(
    stale_ref, q_ref, kv_ref, w_ref, out_ref,
    xall, q_in, kv_in, q_heads, kv, acc, peak, total, result,
    recv, sent, sent_loop, q_recv, q_sent, kv_recv, kv_sent, r_recv, r_sent, local,
):
    row = lax.axis_index("rows")
    part = lax.axis_index("frames")
    core = row % 2
    z = (row // 2) % 4
    y = (row // 8) % 2
    x = row // 16

    def device(x, y, z, core):
        return (((x * 2 + y) * 4 + z) * 2 + core, part)

    def ring(along_first, step):
        dx = step * (1 - core) if along_first else step * core
        dz = step * core if along_first else step * (1 - core)
        return device((x + dx + 4) % 4, y, (z + dz + 4) % 4, core)

    a_up, a_down = ring(True, 1), ring(True, -1)
    b_up, b_down = ring(False, 1), ring(False, -1)
    mate = device(x, y, z, 1 - core)
    across = device(x, 1 - y, z, core)
    quad = [(0, 1, across), (1, 0, mate), (1, 1, device(x, 1 - y, z, 1 - core))]

    barrier = pltpu.get_barrier_semaphore()
    for other in (a_up, a_down, b_up, b_down, across, mate, quad[2][2]):
        pl.semaphore_signal(barrier, inc=1, device_id=other, device_id_type=MESH)
    pl.semaphore_wait(barrier, 7)

    started = []

    def push(src, dst, send_sem, recv_sem, to):
        copy = pltpu.make_async_remote_copy(
            src_ref=src, dst_ref=dst, send_sem=send_sem, recv_sem=recv_sem,
            device_id=to, device_id_type=MESH,
        )
        copy.start()
        return copy

    def send(src, slot, to):
        da, dc, db, dy = slot
        dst = xall.at[da, dc, db] if dy is None else xall.at[da, dc, db, dy]
        started.append(push(src, dst, sent.at[len(started)], recv.at[da, dc, db, dy or 0], to))

    def arrived(da, dc, db, dy=None):
        dst = xall.at[da, dc, db] if dy is None else xall.at[da, dc, db, dy]
        pltpu.make_async_remote_copy(
            src_ref=dst, dst_ref=dst, send_sem=recv.at[da, dc, db, dy or 0],
            recv_sem=recv.at[da, dc, db, dy or 0], device_id=mate, device_id_type=MESH,
        ).wait_recv()

    own = stale_ref.at[y]
    send(stale_ref.at[1 - y], (0, 0, 0, 1), across)
    for slot, to in (
        ((0, 1, 0, 0), mate), ((3, 0, 0, 0), a_up), ((1, 0, 0, 0), a_down),
        ((0, 0, 3, 0), b_up), ((0, 0, 1, 0), b_down),
    ):
        send(own, slot, to)
    keep_own = pltpu.make_async_copy(own, xall.at[0, 0, 0, 0], local.at[0])
    keep_own.start()
    q_copies = []
    for dc, dy, to in quad:
        q_copies.append(push(
            q_ref.at[(y + dy) % 2, (core + dc) % 2], q_in.at[dc * 2 + dy],
            q_sent.at[dc * 2 + dy], q_recv.at[dc * 2 + dy], to,
        ))
    kv_copies = []
    for dc, dy, to in quad:
        kv_copies.append(push(
            kv_ref.at[(y + dy) % 2, (core + dc) % 2], kv_in.at[dc * 2 + dy],
            kv_sent.at[dc * 2 + dy], kv_recv.at[dc * 2 + dy], to,
        ))
    keep_q = pltpu.make_async_copy(q_ref.at[y, core], q_in.at[0], local.at[1])
    keep_q.start()
    keep_kv = pltpu.make_async_copy(kv_ref.at[y, core], kv_in.at[0], local.at[2])
    keep_kv.start()

    arrived(0, 0, 0, 1)
    second = xall.at[0, 0, 0, 1]
    for slot, to in (
        ((0, 1, 0, 1), mate), ((3, 0, 0, 1), a_up), ((1, 0, 0, 1), a_down),
        ((0, 0, 3, 1), b_up), ((0, 0, 1, 1), b_down),
    ):
        send(second, slot, to)

    keep_q.wait()
    for copy in q_copies:
        copy.wait_recv()
    lane = lax.broadcasted_iota(jnp.int32, (QUERIES, 128), 1)
    for pair in range(PAIRS):
        both = q_in[:, :, 128 * pair : 128 * pair + 128].reshape(QUERIES, 128)
        zero = jnp.zeros_like(both)
        q_heads[2 * pair] = jnp.where(lane < HEAD_DIM, both, zero)
        if pair < 2:
            q_heads[2 * pair + 1] = jnp.where(lane < HEAD_DIM, zero, both)
    acc[...] = jnp.zeros_like(acc)
    total[...] = jnp.zeros_like(total)
    peak[...] = jnp.full_like(peak, NEG)
    weight = w_ref.at[core]

    def project(rows, first):
        kv[first : first + rows.shape[0]] = jnp.dot(
            rows, weight[...], preferred_element_type=F32
        ).astype(BF16)

    def attend(keys, masked, hooks):
        for pair in range(PAIRS):
            k = kv[:keys, 128 * pair : 128 * pair + 128]
            v = kv[:keys, HALF + 128 * pair : HALF + 128 * pair + 128]
            factors, parts = [], []
            for head in range(2 * pair, min(2 * pair + 2, 5)):
                s = lax.dot_general(q_heads[head], k, NT, preferred_element_type=F32)
                if masked:
                    q_patch = lax.broadcasted_iota(jnp.int32, (QUERIES, keys), 0) // PATCH
                    k_patch = lax.broadcasted_iota(jnp.int32, (QUERIES, keys), 1) // PATCH
                    drop = ((k_patch < 4) & (k_patch == q_patch)) | (
                        (k_patch >= 4) & (k_patch != q_patch + 4)
                    )
                    s = jnp.where(drop, NEG, s)
                old = peak[head]
                new = jnp.maximum(old, jnp.max(s, axis=1, keepdims=True))
                factor = jnp.exp2(old - new)
                w = jnp.exp2(s - new[:, :1])
                total[head] = total[head] * factor + jnp.sum(w, axis=1, keepdims=True)
                peak[head] = new
                factors.append(factor)
                parts.append(jnp.dot(w.astype(BF16), v, preferred_element_type=F32))
                if head in hooks:
                    hooks[head]()
            if len(parts) == 2:
                acc[pair] = acc[pair] * jnp.where(lane < HEAD_DIM, *factors) + jnp.where(
                    lane < HEAD_DIM, *parts
                )
            else:
                acc[pair] = acc[pair] * factors[0] + parts[0]

    def loop_copies(da):
        plan = (
            (xall.at[da, 0, 3, 0], xall.at[da, 0, 2, 0], recv.at[da, 0, 2, 0], b_up),
            (xall.at[da, 0, 1, 1], xall.at[da, 0, 2, 1], recv.at[da, 0, 2, 1], b_down),
            (xall.at[da, 0, 3], xall.at[da, 1, 3], recv.at[da, 1, 3, 0], mate),
            (xall.at[da, 0, 1], xall.at[da, 1, 1], recv.at[da, 1, 1, 0], mate),
            (xall.at[da, 0, 2], xall.at[da, 1, 2], recv.at[da, 1, 2, 0], mate),
        )
        return [
            pltpu.make_async_remote_copy(
                src_ref=src, dst_ref=dst, send_sem=sent_loop.at[da, i], recv_sem=sem,
                device_id=to, device_id_type=MESH,
            )
            for i, (src, dst, sem, to) in enumerate(plan)
        ]

    def along_b_first(da, split):
        copies = loop_copies(da)
        for db in (3, 1):
            if split:
                arrived(da, 0, db, 0)
                arrived(da, 0, db, 1)
            else:
                arrived(da, 0, db)
        for copy in copies[:4]:
            copy.start()

    def along_b_second(da):
        arrived(da, 0, 2, 0)
        arrived(da, 0, 2, 1)
        loop_copies(da)[4].start()

    def along_a_first():
        for da in (3, 1):
            arrived(da, 0, 0, 0)
            arrived(da, 0, 0, 1)
        send(xall.at[3, 0, 0, 0], (2, 0, 0, 0), a_up)
        send(xall.at[1, 0, 0, 1], (2, 0, 0, 1), a_down)
        for da in (1, 3):
            spread(da)

    def spread(da):
        chunk = xall.at[da, 0, 0]
        send(chunk, (da, 0, 3, None), b_up)
        send(chunk, (da, 0, 1, None), b_down)
        send(chunk, (da, 1, 0, None), mate)

    def along_a_second():
        arrived(2, 0, 0, 0)
        arrived(2, 0, 0, 1)
        spread(2)

    keep_own.wait()
    arrived(0, 1, 0, 0)
    arrived(0, 1, 0, 1)
    for dc in range(2):
        project(xall[0, dc, 0].reshape(2 * PATCH, -1), dc * 2 * PATCH)
    keep_kv.wait()
    for copy in kv_copies:
        copy.wait_recv()
    kv[4 * PATCH : 8 * PATCH] = kv_in[...].reshape(4 * PATCH, -1)
    along_a_first()
    attend(
        8 * PATCH, True,
        {1: lambda: along_b_first(0, True), 2: along_a_second, 3: lambda: along_b_second(0)},
    )

    for db in (3, 1, 2):
        arrived(0, 1, db)
    for dc in range(2):
        project(xall[0, dc, 1:4].reshape(6 * PATCH, -1), dc * 6 * PATCH)
    attend(
        12 * PATCH, False,
        {0: lambda: along_b_first(1, False), 3: lambda: along_b_second(1)},
    )

    def line(da, carry):
        for db in (0, 3, 1, 2):
            arrived(da, 1, db)
        for dc in range(2):
            project(xall[da, dc].reshape(8 * PATCH, -1), dc * 8 * PATCH)

        def more_first():
            @pl.when(da < 3)
            def _():
                along_b_first(da + 1, False)

        def more_second():
            @pl.when(da < 3)
            def _():
                along_b_second(da + 1)

        attend(16 * PATCH, False, {0: more_first, 3: more_second})
        return carry

    lax.fori_loop(1, 4, line, 0)

    for pair in range(PAIRS):
        below = total[2 * pair]
        if pair < 2:
            below = jnp.where(lane < HEAD_DIM, below, total[2 * pair + 1])
        mixed = (acc[pair] / below).astype(BF16)
        result[:, :, 128 * pair : 128 * pair + 128] = mixed.reshape(4, PATCH, 128)
    r_copies = []
    for dc, dy, to in quad:
        r_copies.append(push(
            result.at[dc * 2 + dy], out_ref.at[y, core],
            r_sent.at[dc * 2 + dy], r_recv.at[dc * 2 + dy], to,
        ))
    keep = pltpu.make_async_copy(result.at[0], out_ref.at[y, core], local.at[3])
    keep.start()
    keep.wait()
    for copy in r_copies:
        copy.wait_recv()
    for copy in started + q_copies + kv_copies + r_copies:
        copy.wait_send()
    for da in range(4):
        for copy in loop_copies(da):
            copy.wait_send()


def spatial(stale, q, kv, weight):
    vmem = pl.BlockSpec(memory_space=pltpu.VMEM)
    dma = pltpu.SemaphoreType.DMA
    return pl.pallas_call(
        spatial_kernel,
        out_shape=jax.ShapeDtypeStruct((2, 2, PATCH, HALF), BF16),
        in_specs=[vmem] * 4,
        out_specs=vmem,
        scratch_shapes=[
            pltpu.VMEM((4, 2, 4, 2, PATCH, 640), BF16),
            pltpu.VMEM((4, PATCH, HALF), BF16),
            pltpu.VMEM((4, PATCH, 2 * HALF), BF16),
            pltpu.VMEM((5, QUERIES, 128), BF16),
            pltpu.VMEM((16 * PATCH, 2 * HALF), BF16),
            pltpu.VMEM((PAIRS, QUERIES, 128), F32),
            pltpu.VMEM((5, QUERIES, 128), F32),
            pltpu.VMEM((5, QUERIES, 128), F32),
            pltpu.VMEM((4, PATCH, HALF), BF16),
            dma((4, 2, 4, 2)),
            dma((22,)),
            dma((4, 5)),
            dma((4,)),
            dma((4,)),
            dma((4,)),
            dma((4,)),
            dma((4,)),
            dma((4,)),
            dma((4,)),
        ],
        compiler_params=pltpu.CompilerParams(
            collective_id=0, has_side_effects=True, vmem_limit_bytes=48 << 20
        ),
        name="spatial",
    )(stale, q, kv, weight)


def half_columns(weight):
    count = weight.shape[1] // 640
    split = weight.reshape(640, count, 2, 320)
    split = jnp.pad(split, ((0, 0), (0, 0), (0, 0), (0, 64)))
    return jnp.transpose(split, (2, 0, 1, 3)).reshape(2, 640, count * HALF)


def body(
    latents,
    previous,
    stale_normed,
    norm_gains,
    logit_scale,
    conv_weight,
    attn_weight,
    attn_out,
    temporal_weight,
    temporal_out,
    ff_in,
    ff_out,
):
    frames_here, rows_here, cols_here, width = latents.shape
    padded = extended(previous, (("rows", 1),), 1)
    field = jnp.concatenate([padded[:, :1], latents, padded[:, rows_here + 1 :]], axis=1)
    field = jax.nn.silu(field.astype(F32)).astype(BF16)
    field = jnp.pad(field, ((0, 0), (0, 0), (1, 1), (0, 0)))
    conv_sum = jnp.zeros(latents.shape, F32)
    for row_step in range(3):
        for col_step in range(3):
            window = field[:, row_step : row_step + rows_here, col_step : col_step + cols_here]
            conv_sum = conv_sum + jnp.dot(
                window, conv_weight[row_step * 3 + col_step], preferred_element_type=F32
            )
    first = latents.astype(F32) + conv_sum
    normed = layer_norm(first, norm_gains[0]).reshape(2, PATCH, width)
    halves = half_columns(attn_weight)
    triple = jnp.einsum("fpc,hcd->fhpd", normed, halves, preferred_element_type=F32)
    scale = logit_scale[0] * (math.log2(math.e) / math.sqrt(HEAD_DIM))
    lanes = jnp.pad(jnp.repeat(scale, HEAD_DIM).reshape(2, 320), ((0, 0), (0, 64)))
    q = (triple[..., :HALF] * lanes[None, :, None, :]).astype(BF16)
    kv_now = triple[..., HALF:].astype(BF16)
    mixed = spatial(
        stale_normed.reshape(2, PATCH, width), q, kv_now, halves[:, :, HALF:]
    )
    spatial_mix = jnp.concatenate([mixed[:, 0, :, :320], mixed[:, 1, :, :320]], axis=-1)
    spatial_mix = spatial_mix.reshape(latents.shape)
    second = first + jnp.dot(spatial_mix, attn_out, preferred_element_type=F32)
    normed_two = layer_norm(second, norm_gains[1])
    time_scale = logit_scale[1] / math.sqrt(HEAD_DIM)
    groups = lax.axis_size("frames")
    split_view = normed_two.reshape(frames_here, rows_here, groups, cols_here // groups, width)
    projected = jnp.dot(
        lax.all_to_all(split_view, "frames", split_axis=2, concat_axis=0, tiled=True),
        temporal_weight,
        preferred_element_type=F32,
    ).astype(BF16)
    spread_out = temporal_mix(
        projected[..., :width],
        projected[..., width : 2 * width],
        projected[..., 2 * width :],
        time_scale,
    )
    returned = lax.all_to_all(spread_out, "frames", split_axis=0, concat_axis=2, tiled=True)
    mixed_time = returned.reshape(latents.shape)
    third = second + jnp.dot(mixed_time, temporal_out, preferred_element_type=F32)
    normed_three = layer_norm(third, norm_gains[2])
    both = jnp.dot(normed_three, ff_in, preferred_element_type=F32)
    half = ff_out.shape[0]
    ff_hidden = (both[..., :half] * jax.nn.gelu(both[..., half:], approximate=False)).astype(BF16)
    return third + jnp.dot(ff_hidden, ff_out, preferred_element_type=F32)


def solution(mesh):
    split = P("frames", "rows", None, None)
    return jax.shard_map(
        body,
        mesh=mesh,
        in_specs=(split,) * 3 + (P(),) * 9,
        out_specs=split,
        check_vma=False,
    )
```

```python
import functools
import math

import jax
import jax.numpy as jnp
from jax import lax
from jax.experimental import pallas as pl
from jax.experimental.pallas import tpu as pltpu
from jax.sharding import PartitionSpec as P

HEAD_DIM = 64
NEG = -1e30
EPS = 1e-05
F32 = jnp.float32
BF16 = jnp.bfloat16
MESH = pl.DeviceIdType.MESH
NT = (((1,), (1,)), ((), ()))
WIDTH = 640
COLS = 48
PATCH = 96
QUERIES = 384
HALF = 384
HIDDEN = 2560
FF_STEP = 512
LOG2E = math.log2(math.e)

SLOTS = {
    (1, 0): (0, 0), (3, 0): (0, 1), (0, 1): (0, 2), (0, 3): (0, 3),
    (1, 1): (1, 0), (1, 3): (1, 1), (3, 1): (1, 2), (3, 3): (1, 3),
    (2, 1): (2, 0), (2, 3): (2, 1), (1, 2): (2, 2), (3, 2): (2, 3),
    (0, 0): (3, 0), (2, 0): (3, 1), (0, 2): (3, 2), (2, 2): (3, 3),
}


def dot(left, right):
    return jnp.dot(left, right, preferred_element_type=F32)


def layer_norm(values, gain):
    centre = values - jnp.mean(values, axis=-1, keepdims=True)
    spread = jnp.mean(centre * centre, axis=-1, keepdims=True)
    return (centre * lax.rsqrt(spread + EPS) * gain).astype(BF16)


def block_kernel(
    latents_hbm, previous_hbm, stale_hbm, gains_ref, scale_ref, conv_hbm, attn_hbm, attn_out_hbm,
    time_hbm, time_out_hbm, ff_in_hbm, ff_out_hbm,
    out_ref,
    lat, halo, field, conv_w, wall, attn_out_w, time_w, time_out_w, ff_in_w, ff_out_w,
    first, first_all, q_now, kv_now, xall, q_in, kv_in, q_heads, kv, acc, peak, total,
    result, mixes, time_qkv, time_mix, third, hidden, back, back_in,
    load, recv, sent, q_recv, q_sent, kv_recv, kv_sent, r_recv, r_sent, h_recv, h_sent,
    f_recv, f_sent, local,
):
    row = lax.axis_index("rows")
    part = lax.axis_index("frames")
    core = row % 2
    z = (row // 2) % 4
    y = (row // 8) % 2
    x = row // 16

    def device(x, y, z, core, part=part):
        return (((x * 2 + y) * 4 + z) * 2 + core, part)

    def ring(along_first, step):
        dx = step * (1 - core) if along_first else step * core
        dz = step * core if along_first else step * (1 - core)
        return device((x + dx + 4) % 4, y, (z + dz + 4) % 4, core)

    a_up, a_down = ring(True, 1), ring(True, -1)
    b_up, b_down = ring(False, 1), ring(False, -1)

    def column(dc, dy, part):
        return device(x, (y + dy) % 2, z, (core + dc) % 2, part)

    mate, across = column(1, 0, part), column(0, 1, part)
    quad = [(0, 1, across), (1, 0, mate), (1, 1, column(1, 1, part))]
    partner = (row, 1 - part)

    loads = []

    def fetch(src, dst):
        copy = pltpu.make_async_copy(src, dst, load.at[len(loads)])
        loads.append(copy)
        copy.start()
        return copy

    lat_copy = fetch(latents_hbm, lat)
    conv_copies = [
        fetch(conv_hbm.at[pl.ds(3 * tap, 3)], conv_w.at[pl.ds(3 * tap, 3)]) for tap in (1, 0, 2)
    ]

    barrier = pltpu.get_barrier_semaphore()

    def greet(other):
        pl.semaphore_signal(barrier, inc=1, device_id=other, device_id_type=MESH)

    for other in (a_up, a_down, b_up, b_down) + tuple(item[2] for item in quad):
        greet(other)
    for dc in range(2):
        for dy in range(2):
            greet(column(dc, dy, 1 - part))

    @pl.when(row > 0)
    def _():
        greet((row - 1, part))

    @pl.when(row < 63)
    def _():
        greet((row + 1, part))

    wall_copies = []
    for half in range(2):
        for kind in range(3):
            wall_copies.append(fetch(
                attn_hbm.at[:, pl.ds(WIDTH * kind + 384 * half, 256)],
                wall.at[half, :, pl.ds(HALF * kind, 256)],
            ))
            wall_copies.append(fetch(
                attn_hbm.at[:, pl.ds(WIDTH * kind + 256, 128)],
                wall.at[half, :, pl.ds(HALF * kind + 256, 128)],
            ))
    late_copies = [
        fetch(attn_out_hbm, attn_out_w), fetch(time_hbm, time_w), fetch(time_out_hbm, time_out_w),
        fetch(ff_in_hbm, ff_in_w), fetch(ff_out_hbm, ff_out_w),
    ]

    @pl.when((row > 0) & (row < 63))
    def _():
        pl.semaphore_wait(barrier, 13)

    @pl.when((row == 0) | (row == 63))
    def _():
        pl.semaphore_wait(barrier, 12)

    started = []

    def remote(src, dst, send_sem, recv_sem, to):
        return pltpu.make_async_remote_copy(
            src_ref=src, dst_ref=dst, send_sem=send_sem, recv_sem=recv_sem,
            device_id=to, device_id_type=MESH,
        )

    to_above = remote(previous_hbm.at[:, 0], halo.at[1], h_sent.at[0], h_recv.at[1], (row - 1, part))
    to_below = remote(previous_hbm.at[:, 1], halo.at[0], h_sent.at[1], h_recv.at[0], (row + 1, part))

    @pl.when(row > 0)
    def _():
        to_above.start()

    @pl.when(row < 63)
    def _():
        to_below.start()

    def send(src, at, to, dc=0, dy=None, places=1):
        group, place = SLOTS[at]
        if dy is not None:
            dst = xall.at[group, dc, place, dy]
        else:
            dst = xall.at[group, dc, pl.ds(place, places)]
        copy = remote(
            src, dst, sent.at[len(started)], recv.at[group, dc, place, dy or 0], to
        )
        started.append(copy)
        return copy

    def arrival(at, dc=0, dy=None, places=1):
        group, place = SLOTS[at]
        if dy is not None:
            dst = xall.at[group, dc, place, dy]
        else:
            dst = xall.at[group, dc, pl.ds(place, places)]
        sem = recv.at[group, dc, place, dy or 0]
        return lambda: remote(dst, dst, sem, sem, mate).wait_recv()

    def held(at, dy=None, places=1):
        group, place = SLOTS[at]
        if dy is not None:
            return xall.at[group, 0, place, dy]
        return xall.at[group, 0, pl.ds(place, places)]

    def arrive(at, dc=0, dy=None, places=1):
        arrival(at, dc, dy, places)()

    def own_ways(src, dy):
        return [
            send(src, (3, 0), a_up, dy=dy), send(src, (1, 0), a_down, dy=dy),
            send(src, (0, 3), b_up, dy=dy), send(src, (0, 1), b_down, dy=dy),
            send(src, (0, 0), mate, dc=1, dy=dy),
        ]

    def start(copies):
        for copy in copies:
            copy.start()

    own = stale_hbm.at[y]
    start([send(stale_hbm.at[1 - y], (0, 0), across, dy=1)])
    start(own_ways(own, 0))
    keep_own = pltpu.make_async_copy(own, held((0, 0), 0), local.at[0])
    keep_own.start()

    neighbours_a = [
        send(held((3, 0), 0), (2, 0), a_up, dy=0), send(held((1, 0), 1), (2, 0), a_down, dy=1),
        send(held((1, 0)), (1, 3), b_up), send(held((1, 0)), (1, 1), b_down),
        send(held((3, 0)), (3, 3), b_up), send(held((3, 0)), (3, 1), b_down),
        send(held((1, 0), places=2), (1, 0), mate, dc=1, places=2),
    ]

    def along_b(da, places):
        copies = [
            send(held((da, 3), 0), (da, 2), b_up, dy=0),
            send(held((da, 1), 1), (da, 2), b_down, dy=1),
        ]
        return copies + [send(held((da, 1), places=2), (da, 1), mate, dc=1, places=2)]

    on_b = {da: along_b(da, 2) for da in range(4)}
    far_a = [
        send(held((2, 0)), (2, 3), b_up), send(held((2, 0)), (2, 1), b_down),
        send(held((2, 0)), (2, 0), mate, dc=1),
    ]
    far_b = [send(held((0, 2)), (0, 2), mate, dc=1)]
    far_lines = [send(held((1, 2), places=2), (1, 2), mate, dc=1, places=2)]
    corner = [send(held((2, 2)), (2, 2), mate, dc=1)]
    dy_ways = own_ways(held((0, 0), 1), 1)

    def own_second():
        arrive((0, 0), dy=1)
        start(dy_ways)

    def near():
        for dy in range(2):
            arrive((1, 0), dy=dy)
            arrive((3, 0), dy=dy)
        start(neighbours_a)
        for dy in range(2):
            arrive((0, 1), dy=dy)
            arrive((0, 3), dy=dy)
        start(on_b[0])

    def far_first():
        for dy in range(2):
            arrive((2, 0), dy=dy)
        start(far_a)

    def far_second():
        for dy in range(2):
            arrive((0, 2), dy=dy)
        start(far_b)

    def line(da):
        arrive((da, 1))
        arrive((da, 3))
        start(on_b[da])

    def lines_far():
        for da in (1, 3):
            for dy in range(2):
                arrive((da, 2), dy=dy)
        start(far_lines)

    def last_corner():
        for dy in range(2):
            arrive((2, 2), dy=dy)
        start(corner)

    column_at = lax.broadcasted_iota(jnp.int32, (COLS, WIDTH), 0)

    def fill(at, values):
        for frame in range(2):
            cells = values[frame].astype(F32)
            cells = cells * (1.0 / (1.0 + jnp.exp(-cells)))
            left = jnp.where(column_at == 0, 0.0, pltpu.roll(cells, 1, 0))
            right = jnp.where(column_at == COLS - 1, 0.0, pltpu.roll(cells, COLS - 1, 0))
            field[frame, at, :, :WIDTH] = left.astype(BF16)
            field[frame, at, :, WIDTH : 2 * WIDTH] = cells.astype(BF16)
            field[frame, at, :, 2 * WIDTH :] = right.astype(BF16)

    def taps(at):
        return dot(
            field[:, at : at + 2].reshape(2 * PATCH, 3 * WIDTH),
            conv_w[3 * at : 3 * at + 3].reshape(3 * WIDTH, WIDTH),
        )

    lat_copy.wait()
    fill(1, lat[:, 0])
    fill(2, lat[:, 1])
    conv_copies[0].wait()
    conv_sum = taps(1)
    own_second()

    @pl.when(row > 0)
    def _():
        to_below.wait_recv()

    @pl.when(row == 0)
    def _():
        halo[0] = jnp.zeros_like(halo[0])

    @pl.when(row < 63)
    def _():
        to_above.wait_recv()

    @pl.when(row == 63)
    def _():
        halo[1] = jnp.zeros_like(halo[1])

    fill(0, halo[0])
    fill(3, halo[1])
    conv_copies[1].wait()
    conv_sum = conv_sum + taps(0)
    conv_copies[2].wait()
    conv_sum = conv_sum + taps(2)
    start_sum = lat[...].reshape(2 * PATCH, WIDTH).astype(F32) + conv_sum
    parts = start_sum.reshape(2, 2, COLS, WIDTH)
    first[0] = parts[:, 0]
    first[1] = parts[:, 1]
    first_copy = remote(
        first.at[1 - part], first_all.at[part], f_sent.at[0], f_recv.at[0], partner
    )
    first_copy.start()
    normed = layer_norm(start_sum, gains_ref[0:1, :])
    for copy in wall_copies:
        copy.wait()
    lane = lax.broadcasted_iota(jnp.int32, (QUERIES, 128), 1)
    half_lane = lax.broadcasted_iota(jnp.int32, (1, 128), 1) // HEAD_DIM

    def lane_scale(kind, pair):
        low, high = scale_ref[kind, 2 * pair], scale_ref[kind, 2 * pair + 1]
        return jnp.where(half_lane == 0, low, high) * (LOG2E / math.sqrt(HEAD_DIM))

    for half in range(2):
        triple = dot(normed, wall[half]).reshape(2, PATCH, 3 * HALF)
        for place, pair in enumerate((3 * half, 3 * half + 1, 2)):
            lanes = slice(128 * place, 128 * place + 128)
            q_now[:, half, :, lanes] = (triple[..., lanes] * lane_scale(0, pair)).astype(BF16)
        kv_now[:, half] = triple[..., HALF:].astype(BF16)
    q_copies, kv_copies = [], []
    for dc, dy, to in quad:
        at = dc * 2 + dy
        q_copies.append(remote(
            q_now.at[(y + dy) % 2, (core + dc) % 2], q_in.at[at], q_sent.at[at], q_recv.at[at], to
        ))
        kv_copies.append(remote(
            kv_now.at[(y + dy) % 2, (core + dc) % 2], kv_in.at[at], kv_sent.at[at],
            kv_recv.at[at], to,
        ))
    start(q_copies)
    start(kv_copies)
    q_in[0] = q_now[y, core]
    kv_in[0] = kv_now[y, core]
    near()
    keep_own.wait()
    arrive((0, 0), dc=1, dy=0)
    arrive((0, 0), dc=1, dy=1)

    def project(rows, at):
        count = rows.shape[0] * rows.shape[1] * rows.shape[2] * rows.shape[3]
        kv[at : at + count] = dot(
            rows.reshape(count, WIDTH), wall[core, :, HALF:]
        ).astype(BF16)

    for dc in range(2):
        project(xall[3, dc, 0:1], dc * 2 * PATCH)

    for copy in q_copies:
        copy.wait_recv()
    for pair in range(3):
        both = q_in[:, :, 128 * pair : 128 * pair + 128].reshape(QUERIES, 128)
        zero = jnp.zeros_like(both)
        if pair < 2:
            q_heads[2 * pair] = jnp.where(lane < HEAD_DIM, both, zero)
            q_heads[2 * pair + 1] = jnp.where(lane < HEAD_DIM, zero, both)
        else:
            q_heads[4] = jnp.where(lane // HEAD_DIM == core, both, zero)
    acc[...] = jnp.zeros_like(acc)
    total[...] = jnp.zeros_like(total)
    peak[...] = jnp.full_like(peak, NEG)

    def attend(keys, masked, hooks):
        for pair in range(3):
            k = kv[:keys, 128 * pair : 128 * pair + 128]
            v = kv[:keys, HALF + 128 * pair : HALF + 128 * pair + 128]
            factors, sums = [], []
            for head in range(2 * pair, min(2 * pair + 2, 5)):
                s = lax.dot_general(q_heads[head], k, NT, preferred_element_type=F32)
                if masked:
                    q_patch = lax.broadcasted_iota(jnp.int32, (QUERIES, keys), 0) // PATCH
                    k_patch = lax.broadcasted_iota(jnp.int32, (QUERIES, keys), 1) // PATCH
                    drop = ((k_patch < 4) & (k_patch == q_patch)) | (
                        (k_patch >= 4) & (k_patch != q_patch + 4)
                    )
                    s = jnp.where(drop, NEG, s)
                old = peak[head]
                new = jnp.maximum(old, jnp.max(s, axis=1, keepdims=True))
                factor = jnp.exp2(old - new)
                w = jnp.exp2(s - new[:, :1])
                total[head] = total[head] * factor + jnp.sum(w, axis=1, keepdims=True)
                peak[head] = new
                factors.append(factor)
                sums.append(dot(w.astype(BF16), v))
                if head in hooks:
                    hooks[head]()
            if len(sums) == 2:
                acc[pair] = acc[pair] * jnp.where(lane < HEAD_DIM, *factors) + jnp.where(
                    lane < HEAD_DIM, *sums
                )
            else:
                acc[pair] = acc[pair] * factors[0] + sums[0]

    for copy in kv_copies:
        copy.wait_recv()
    kv[4 * PATCH : 8 * PATCH] = kv_in[...].reshape(4 * PATCH, 2 * HALF)
    attend(8 * PATCH, True, {2: far_first})

    def group(g, carry):
        def when(table):
            def hook():
                for at, actions in table.items():
                    @pl.when(g == at)
                    def _():
                        for action in actions:
                            action()
            return hook

        when({
            0: [arrival((1, 0), 1, None, 2), arrival((0, 1), 1, None, 2)],
            1: [arrival((1, 1), 1, None, 2), arrival((3, 1), 1, None, 2)],
            2: [arrival((2, 1), 1, None, 2), arrival((1, 2), 1, None, 2)],
        })()
        for dc in range(2):
            project(xall[g, dc], dc * 8 * PATCH)
        attend(16 * PATCH, False, {
            0: when({0: [functools.partial(line, 1)]}),
            1: when({0: [functools.partial(line, 3)]}),
            2: when({0: [far_second], 1: [functools.partial(line, 2)], 2: [last_corner]}),
            4: when({1: [lines_far]}),
        })
        return carry

    lax.fori_loop(0, 3, group, 0)
    arrive((2, 0), 1)
    arrive((0, 2), 1)
    arrive((2, 2), 1)
    for dc in range(2):
        project(xall[3, dc, 1:4], dc * 6 * PATCH)
    attend(12 * PATCH, False, {})

    for pair in range(3):
        below = total[2 * pair]
        if pair < 2:
            below = jnp.where(lane < HEAD_DIM, below, total[2 * pair + 1])
        mixed = acc[pair] / below
        if pair == 2:
            mixed = jnp.where(lane // HEAD_DIM == core, mixed, 0.0)
        result[:, :, :, 128 * pair : 128 * pair + 128] = mixed.astype(BF16).reshape(4, 2, COLS, 128)
    r_copies = []
    for flip in (1, 0):
        for dc in range(2):
            for dy in range(2):
                if flip + dc + dy == 0:
                    continue
                to_part = part + flip - 2 * part * flip
                at = 4 * flip + 2 * dc + dy
                r_copies.append(remote(
                    result.at[2 * dc + dy, to_part], mixes.at[2 * part + y, core],
                    r_sent.at[at], r_recv.at[at], column(dc, dy, to_part),
                ))
    start(r_copies)
    mixes[2 * part + y, core] = result[0, part]
    first_all[part] = first[part]
    first_copy.wait_recv()
    for copy in late_copies:
        copy.wait()
    for copy in r_copies:
        copy.wait_recv()

    rows = 4 * COLS
    middle = mixes[:, 0, :, 256:] + mixes[:, 1, :, 256:]
    mix = jnp.concatenate(
        [mixes[:, 0, :, :256], middle, mixes[:, 1, :, :256]], axis=-1
    ).reshape(rows, WIDTH)
    second = first_all[...].reshape(rows, WIDTH) + dot(mix, attn_out_w[...])
    third[...] = second
    time_qkv[...] = dot(layer_norm(second, gains_ref[1:2, :]), time_w[...]).astype(BF16)

    ones_row = lax.broadcasted_iota(jnp.int32, (256, 128), 0) % 128 // HEAD_DIM
    ones_col = lax.broadcasted_iota(jnp.int32, (256, 128), 1) // HEAD_DIM
    ones = jnp.where(ones_row == ones_col, 1.0, 0.0).astype(BF16)
    for pair in range(5):
        def lanes_of(kind):
            at = WIDTH * kind + 128 * pair
            return time_qkv[:, at : at + 128].reshape(4, COLS, 128).astype(F32)

        tq, tk, tv = lanes_of(0), lanes_of(1), lanes_of(2)
        products = (tq[:, None] * tk[None]).reshape(16 * COLS, 128)
        high = products.astype(BF16)
        low = (products - high.astype(F32)).astype(BF16)
        s = dot(jnp.concatenate([high, low], axis=1), ones) * lane_scale(1, pair)
        s = s.reshape(4, 4, COLS, 128)
        w = jnp.exp2(s - jnp.max(s, axis=1, keepdims=True))
        mixed = jnp.sum(w.astype(BF16).astype(F32) * tv[None], axis=1) / jnp.sum(w, axis=1)
        time_mix[:, 128 * pair : 128 * pair + 128] = mixed.astype(BF16).reshape(rows, 128)
    third[...] = third[...] + dot(time_mix[...], time_out_w[...])
    normed_three = layer_norm(third[...], gains_ref[2:3, :])
    for step in range(HIDDEN // FF_STEP):
        at = FF_STEP * step
        value = dot(normed_three, ff_in_w[:, at : at + FF_STEP])
        gate = dot(normed_three, ff_in_w[:, HIDDEN + at : HIDDEN + at + FF_STEP])
        gelu = 0.5 * gate * (1.0 + lax.erf(gate * math.sqrt(0.5)))
        hidden[:, at : at + FF_STEP] = (value * gelu).astype(BF16)
    done = third[...] + dot(hidden[...], ff_out_w[...])
    third[...] = done
    half_rows = 2 * COLS
    back[...] = third[pl.ds(pl.multiple_of((1 - part) * half_rows, half_rows), half_rows)].astype(BF16)
    back_copy = remote(back, back_in, f_sent.at[1], f_recv.at[1], partner)
    back_copy.start()
    mine = third[pl.ds(pl.multiple_of(part * half_rows, half_rows), half_rows)]
    out_ref[:, part] = mine.reshape(2, COLS, WIDTH)
    back_copy.wait_recv()
    out_ref[:, 1 - part] = back_in[...].astype(F32).reshape(2, COLS, WIDTH)
    for copy in started + q_copies + kv_copies + r_copies + [first_copy, back_copy]:
        copy.wait_send()

    @pl.when(row > 0)
    def _():
        to_above.wait_send()

    @pl.when(row < 63)
    def _():
        to_below.wait_send()


def body(*arrays):
    vmem = pl.BlockSpec(memory_space=pltpu.VMEM)
    hbm = pl.BlockSpec(memory_space=pl.ANY)
    dma = pltpu.SemaphoreType.DMA
    rows = 4 * COLS
    return pl.pallas_call(
        block_kernel,
        out_shape=jax.ShapeDtypeStruct((2, 2, COLS, WIDTH), F32),
        in_specs=[hbm] * 3 + [vmem, pl.BlockSpec(memory_space=pltpu.SMEM)] + [hbm] * 7,
        out_specs=vmem,
        scratch_shapes=[
            pltpu.VMEM((2, 2, COLS, WIDTH), BF16),
            pltpu.VMEM((2, 2, COLS, WIDTH), BF16),
            pltpu.VMEM((2, 4, COLS, 3 * WIDTH), BF16),
            pltpu.VMEM((9, WIDTH, WIDTH), BF16),
            pltpu.VMEM((2, WIDTH, 3 * HALF), BF16),
            pltpu.VMEM((WIDTH, WIDTH), BF16),
            pltpu.VMEM((WIDTH, 3 * WIDTH), BF16),
            pltpu.VMEM((WIDTH, WIDTH), BF16),
            pltpu.VMEM((WIDTH, 2 * HIDDEN), BF16),
            pltpu.VMEM((HIDDEN, WIDTH), BF16),
            pltpu.VMEM((2, 2, COLS, WIDTH), F32),
            pltpu.VMEM((2, 2, COLS, WIDTH), F32),
            pltpu.VMEM((2, 2, PATCH, HALF), BF16),
            pltpu.VMEM((2, 2, PATCH, 2 * HALF), BF16),
            pltpu.VMEM((4, 2, 4, 2, 2, COLS, WIDTH), BF16),
            pltpu.VMEM((4, PATCH, HALF), BF16),
            pltpu.VMEM((4, PATCH, 2 * HALF), BF16),
            pltpu.VMEM((5, QUERIES, 128), BF16),
            pltpu.VMEM((16 * PATCH, 2 * HALF), BF16),
            pltpu.VMEM((3, QUERIES, 128), F32),
            pltpu.VMEM((5, QUERIES, 128), F32),
            pltpu.VMEM((5, QUERIES, 128), F32),
            pltpu.VMEM((4, 2, COLS, HALF), BF16),
            pltpu.VMEM((4, 2, COLS, HALF), BF16),
            pltpu.VMEM((rows, 3 * WIDTH), BF16),
            pltpu.VMEM((rows, WIDTH), BF16),
            pltpu.VMEM((rows, WIDTH), F32),
            pltpu.VMEM((rows, HIDDEN), BF16),
            pltpu.VMEM((PATCH, WIDTH), BF16),
            pltpu.VMEM((PATCH, WIDTH), BF16),
            dma((21,)),
            dma((4, 2, 4, 2)),
            dma((36,)),
            dma((4,)),
            dma((4,)),
            dma((4,)),
            dma((4,)),
            dma((8,)),
            dma((8,)),
            dma((2,)),
            dma((2,)),
            dma((2,)),
            dma((2,)),
            dma((1,)),
        ],
        compiler_params=pltpu.CompilerParams(
            collective_id=0, has_side_effects=True, vmem_limit_bytes=62 << 20
        ),
        name="block",
    )(*arrays)


def solution(mesh):
    split = P("frames", "rows", None, None)
    return jax.shard_map(
        body,
        mesh=mesh,
        in_specs=(split,) * 3 + (P(),) * 9,
        out_specs=split,
        check_vma=False,
    )
```

```python
import functools
import math

import jax
import jax.numpy as jnp
from jax import lax
from jax.experimental import pallas as pl
from jax.experimental.pallas import tpu as pltpu
from jax.sharding import PartitionSpec as P

HEAD_DIM = 64
NEG = -1e30
EPS = 1e-05
F32 = jnp.float32
BF16 = jnp.bfloat16
MESH = pl.DeviceIdType.MESH
NT = (((1,), (1,)), ((), ()))
WIDTH = 640
COLS = 48
PATCH = 96
QUERIES = 384
HALF = 384
HIDDEN = 2560
FF_STEP = 512
LOG2E = math.log2(math.e)

SLOTS = {
    (1, 0): (0, 0), (3, 0): (0, 1), (0, 1): (0, 2), (0, 3): (0, 3),
    (1, 1): (1, 0), (1, 3): (1, 1), (3, 1): (1, 2), (3, 3): (1, 3),
    (2, 1): (2, 0), (2, 3): (2, 1), (1, 2): (2, 2), (3, 2): (2, 3),
    (0, 0): (3, 0), (2, 0): (3, 1), (0, 2): (3, 2), (2, 2): (3, 3),
}


def dot(left, right):
    return jnp.dot(left, right, preferred_element_type=F32)


def layer_norm(values, gain):
    centre = values - jnp.mean(values, axis=-1, keepdims=True)
    spread = jnp.mean(centre * centre, axis=-1, keepdims=True)
    return (centre * lax.rsqrt(spread + EPS) * gain).astype(BF16)


def block_kernel(
    latents_hbm, previous_hbm, stale_hbm, gains_ref, scale_ref, conv_hbm, attn_hbm, attn_out_hbm,
    time_hbm, time_out_hbm, ff_in_hbm, ff_out_hbm,
    out_ref,
    lat, halo, field, conv_w, wall, attn_out_w, time_w, time_out_w, ff_in_w, ff_out_w,
    first, first_all, norm_in, kv_now, xall, q_heads, kv, scores, top, acc, peak, total,
    result, mixes, time_qkv, time_mix, third, hidden, back, back_in,
    load, recv, sent, n_recv, n_sent, r_recv, r_sent, h_recv, h_sent, l_recv, l_sent,
    f_recv, f_sent, b_recv, b_sent, local,
):
    row = lax.axis_index("rows")
    part = lax.axis_index("frames")
    core = row % 2
    z = (row // 2) % 4
    y = (row // 8) % 2
    x = row // 16

    def device(x, y, z, core, part=part):
        return (((x * 2 + y) * 4 + z) * 2 + core, part)

    def ring(along_first, step):
        dx = step * (1 - core) if along_first else step * core
        dz = step * core if along_first else step * (1 - core)
        return device((x + dx + 4) % 4, y, (z + dz + 4) % 4, core)

    a_up, a_down = ring(True, 1), ring(True, -1)
    b_up, b_down = ring(False, 1), ring(False, -1)

    def column(dc, dy, part):
        return device(x, (y + dy) % 2, z, (core + dc) % 2, part)

    mate, across = column(1, 0, part), column(0, 1, part)
    quad = [(0, 1, across), (1, 0, mate), (1, 1, column(1, 1, part))]
    partner = (row, 1 - part)
    patches = (row, row + 8 - 16 * y)

    loads = []

    def fetch(src, dst):
        copy = pltpu.make_async_copy(src, dst, load.at[len(loads)])
        loads.append(copy)
        copy.start()
        return copy

    lat_copy = fetch(latents_hbm.at[y], lat.at[0])
    conv_copies = [
        fetch(conv_hbm.at[pl.ds(3 * tap, 3)], conv_w.at[pl.ds(3 * tap, 3)]) for tap in (1, 0, 2)
    ]

    barrier = pltpu.get_barrier_semaphore()

    def greet(other):
        pl.semaphore_signal(barrier, inc=1, device_id=other, device_id_type=MESH)

    for other in (a_up, a_down, b_up, b_down) + tuple(item[2] for item in quad):
        greet(other)
    for dc in range(2):
        for dy in range(2):
            greet(column(dc, dy, 1 - part))

    for patch in patches:
        @pl.when(patch > 0)
        def _():
            greet((patch - 1, part))

        @pl.when(patch < 63)
        def _():
            greet((patch + 1, part))

    wall_copies = []
    for kind in range(3):
        wall_copies.append(fetch(
            attn_hbm.at[:, pl.ds(pl.multiple_of(WIDTH * kind + 384 * core, 128), 256)],
            wall.at[:, pl.ds(HALF * kind, 256)],
        ))
        wall_copies.append(fetch(
            attn_hbm.at[:, pl.ds(WIDTH * kind + 256, 128)],
            wall.at[:, pl.ds(HALF * kind + 256, 128)],
        ))
    late_copies = [
        fetch(attn_out_hbm, attn_out_w), fetch(time_hbm, time_w), fetch(time_out_hbm, time_out_w),
        fetch(ff_in_hbm, ff_in_w), fetch(ff_out_hbm, ff_out_w),
    ]

    @pl.when((row > 0) & (row < 63))
    def _():
        pl.semaphore_wait(barrier, 15)

    @pl.when((row == 0) | (row == 63))
    def _():
        pl.semaphore_wait(barrier, 13)

    started = []

    def remote(src, dst, send_sem, recv_sem, to):
        return pltpu.make_async_remote_copy(
            src_ref=src, dst_ref=dst, send_sem=send_sem, recv_sem=recv_sem,
            device_id=to, device_id_type=MESH,
        )

    lat_remote = remote(latents_hbm.at[1 - y], lat.at[1], l_sent.at[0], l_recv.at[0], across)
    lat_remote.start()
    edges = []
    for side in range(2):
        patch = row - 1 + 2 * side
        for frame in range(2):
            to = device(patch // 16, frame, (patch // 2) % 4, patch % 2)
            dy = ((patch // 8) % 2 + frame) % 2
            edges.append(remote(
                previous_hbm.at[frame, side], halo.at[dy, 1 - side],
                h_sent.at[side, frame], h_recv.at[dy, 1 - side], to,
            ))

    @pl.when(row > 0)
    def _():
        edges[0].start()
        edges[1].start()

    @pl.when(row < 63)
    def _():
        edges[2].start()
        edges[3].start()

    def send(src, at, to, dc=0, dy=None, places=1):
        group, place = SLOTS[at]
        if dy is not None:
            dst = xall.at[group, dc, place, dy]
        else:
            dst = xall.at[group, dc, pl.ds(place, places)]
        copy = remote(
            src, dst, sent.at[len(started)], recv.at[group, dc, place, dy or 0], to
        )
        started.append(copy)
        return copy

    def arrival(at, dc=0, dy=None, places=1):
        group, place = SLOTS[at]
        if dy is not None:
            dst = xall.at[group, dc, place, dy]
        else:
            dst = xall.at[group, dc, pl.ds(place, places)]
        sem = recv.at[group, dc, place, dy or 0]
        return lambda: remote(dst, dst, sem, sem, mate).wait_recv()

    def held(at, dy=None, places=1):
        group, place = SLOTS[at]
        if dy is not None:
            return xall.at[group, 0, place, dy]
        return xall.at[group, 0, pl.ds(place, places)]

    def arrive(at, dc=0, dy=None, places=1):
        arrival(at, dc, dy, places)()

    def own_ways(src, dy):
        return [
            send(src, (3, 0), a_up, dy=dy), send(src, (1, 0), a_down, dy=dy),
            send(src, (0, 3), b_up, dy=dy), send(src, (0, 1), b_down, dy=dy),
            send(src, (0, 0), mate, dc=1, dy=dy),
        ]

    def start(copies):
        for copy in copies:
            copy.start()

    own = stale_hbm.at[y]
    start([send(stale_hbm.at[1 - y], (0, 0), across, dy=1)])
    start(own_ways(own, 0))
    keep_own = pltpu.make_async_copy(own, held((0, 0), 0), local.at[0])
    keep_own.start()

    near_a = [
        [send(held((3, 0), 0), (2, 0), a_up, dy=0)], [send(held((1, 0), 1), (2, 0), a_down, dy=1)]
    ]
    near_b = [
        [send(held((0, 3), 0), (0, 2), b_up, dy=0)], [send(held((0, 1), 1), (0, 2), b_down, dy=1)]
    ]
    lines_b = {
        (da, dy): [
            send(held((da, 0), dy), (da, 3), b_up, dy=dy),
            send(held((da, 0), dy), (da, 1), b_down, dy=dy),
        ]
        for da in (1, 3, 2) for dy in range(2)
    }
    ahead = {
        da: [
            send(held((da, 3), 0), (da, 2), b_up, dy=0),
            send(held((da, 1), 1), (da, 2), b_down, dy=1),
        ]
        for da in (1, 3, 2)
    }
    to_mate = {
        at: [send(held(at, places=count), at, mate, dc=1, places=count)]
        for at, count in (
            ((1, 0), 2), ((0, 1), 2), ((1, 1), 2), ((3, 1), 2), ((2, 1), 2), ((1, 2), 2),
            ((2, 0), 1), ((0, 2), 1), ((2, 2), 1),
        )
    }
    dy_ways = own_ways(held((0, 0), 1), 1)

    def own_second():
        arrive((0, 0), dy=1)
        start(dy_ways)

    def near(dy):
        for da in (3, 1):
            arrive((da, 0), dy=dy)
        start(near_a[dy])
        for da in (1, 3):
            start(lines_b[da, dy])
        for db in (3, 1):
            arrive((0, db), dy=dy)
        start(near_b[dy])
        if dy == 1:
            start(to_mate[1, 0])
            start(to_mate[0, 1])

    def far_first():
        for dy in range(2):
            arrive((2, 0), dy=dy)
            start(lines_b[2, dy])
        start(to_mate[2, 0])

    def far_second():
        for dy in range(2):
            arrive((0, 2), dy=dy)
        start(to_mate[0, 2])

    def line(da):
        arrive((da, 3), dy=0)
        arrive((da, 1), dy=1)
        start(ahead[da])
        arrive((da, 3), dy=1)
        arrive((da, 1), dy=0)
        start(to_mate[da, 1])

    def lines_far():
        for da in (1, 3):
            for dy in range(2):
                arrive((da, 2), dy=dy)
        start(to_mate[1, 2])

    def last_corner():
        for dy in range(2):
            arrive((2, 2), dy=dy)
        start(to_mate[2, 2])

    column_at = lax.broadcasted_iota(jnp.int32, (COLS, WIDTH), 0)

    def fill(dy, at, values):
        cells = values.astype(F32)
        cells = cells * (1.0 / (1.0 + jnp.exp(-cells)))
        left = jnp.where(column_at == 0, 0.0, pltpu.roll(cells, 1, 0))
        right = jnp.where(column_at == COLS - 1, 0.0, pltpu.roll(cells, COLS - 1, 0))
        field[dy, at, :, :WIDTH] = left.astype(BF16)
        field[dy, at, :, WIDTH : 2 * WIDTH] = cells.astype(BF16)
        field[dy, at, :, 2 * WIDTH :] = right.astype(BF16)

    def taps(at):
        return dot(
            field[:, at : at + 2].reshape(2 * PATCH, 3 * WIDTH),
            conv_w[3 * at : 3 * at + 3].reshape(3 * WIDTH, WIDTH),
        )

    lat_copy.wait()
    fill(0, 1, lat[0, 0])
    fill(0, 2, lat[0, 1])
    for dy in range(2):
        for side in range(2):
            there = patches[dy] > 0 if side == 0 else patches[dy] < 63
            gone = patches[dy] == 0 if side == 0 else patches[dy] == 63
            edge = halo.at[dy, side]
            sem = h_recv.at[dy, side]

            @pl.when(there)
            def _():
                remote(edge, edge, sem, sem, mate).wait_recv()

            @pl.when(gone)
            def _():
                halo[dy, side] = jnp.zeros_like(halo[dy, side])

            fill(dy, 3 * side, halo[dy, side])
    lat_remote.wait_recv()
    fill(1, 1, lat[1, 0])
    fill(1, 2, lat[1, 1])
    near(0)
    own_second()
    conv_copies[0].wait()
    conv_sum = taps(1)
    conv_copies[1].wait()
    conv_sum = conv_sum + taps(0)
    conv_copies[2].wait()
    conv_sum = conv_sum + taps(2)
    start_sum = lat[...].reshape(2 * PATCH, WIDTH).astype(F32) + conv_sum
    norm_in[0] = layer_norm(start_sum, gains_ref[0:1, :]).reshape(2, PATCH, WIDTH)
    norm_copy = remote(norm_in.at[0], norm_in.at[1], n_sent.at[0], n_recv.at[0], mate)
    norm_copy.start()
    first[...] = start_sum.reshape(2, 2, COLS, WIDTH)
    frame_here = 2 * part + y
    f_copies = []
    for dy, flip in ((0, 1), (1, 0), (1, 1)):
        to_part = part + flip - 2 * part * flip
        at = 2 * dy + flip
        f_copies.append(remote(
            first.at[dy, to_part], first_all.at[frame_here], f_sent.at[at], f_recv.at[at],
            column(0, dy, to_part),
        ))
    start(f_copies)
    first_all[frame_here] = first[0, part]
    for copy in wall_copies:
        copy.wait()
    lane = lax.broadcasted_iota(jnp.int32, (QUERIES, 128), 1)
    half_lane = lax.broadcasted_iota(jnp.int32, (1, 128), 1) // HEAD_DIM

    def lane_scale(kind, pair):
        low, high = scale_ref[kind, 2 * pair], scale_ref[kind, 2 * pair + 1]
        return jnp.where(half_lane == 0, low, high) * (LOG2E / math.sqrt(HEAD_DIM))

    def project(rows, at):
        count = rows.shape[0] * rows.shape[1] * rows.shape[2] * rows.shape[3]
        kv[at : at + count] = dot(rows.reshape(count, WIDTH), wall[:, HALF:]).astype(BF16)

    keep_own.wait()
    arrive((0, 0), dc=1, dy=0)
    arrive((0, 0), dc=1, dy=1)
    for dc in range(2):
        project(xall[3, dc, 0:1], dc * 2 * PATCH)

    norm_copy.wait_recv()
    triple = dot(norm_in[...].reshape(QUERIES, WIDTH), wall[...])
    kv_now[...] = triple[:, HALF:].astype(BF16)
    for place, pair in enumerate((3 * core, 3 * core + 1, 2)):
        both = triple[:, 128 * place : 128 * place + 128] * lane_scale(0, pair)
        both = both.astype(BF16)
        zero = jnp.zeros_like(both)
        if place < 2:
            q_heads[2 * place] = jnp.where(lane < HEAD_DIM, both, zero)
            q_heads[2 * place + 1] = jnp.where(lane < HEAD_DIM, zero, both)
        else:
            q_heads[4] = jnp.where(lane // HEAD_DIM == core, both, zero)
    acc[...] = jnp.zeros_like(acc)
    total[...] = jnp.zeros_like(total)
    peak[...] = jnp.full_like(peak, NEG)

    def attend(keys, masked, hooks):
        def keys_of(head):
            at = 128 * (head // 2)
            return kv[:keys, at : at + 128]

        def score(head):
            s = lax.dot_general(q_heads[head], keys_of(head), NT, preferred_element_type=F32)
            if masked:
                q_patch = lax.broadcasted_iota(jnp.int32, (QUERIES, keys), 0) // PATCH
                k_patch = lax.broadcasted_iota(jnp.int32, (QUERIES, keys), 1) // PATCH
                drop = ((k_patch < 4) & (k_patch == q_patch)) | (
                    (k_patch >= 4) & (k_patch != q_patch + 4)
                )
                s = jnp.where(drop, NEG, s)
            scores[head % 2, :, :keys] = s
            top[head % 2] = jnp.broadcast_to(jnp.max(s, axis=1, keepdims=True), (QUERIES, 128))

        score(0)
        for head in range(5):
            if head in hooks:
                hooks[head]()
            if head < 4:
                score(head + 1)
            pair = head // 2
            old = peak[head]
            new = jnp.maximum(old, top[head % 2])
            factor = jnp.exp2(old - new)
            peak[head] = new
            w = jnp.exp2(scores[head % 2, :, :keys] - new[:, :1])
            total[head] = total[head] * factor + jnp.sum(w, axis=1, keepdims=True)
            at = HALF + 128 * pair
            part_sum = dot(w.astype(BF16), kv[:keys, at : at + 128])
            if head == 4:
                acc[pair] = acc[pair] * factor + part_sum
            else:
                here = (lane < HEAD_DIM) if head % 2 == 0 else (lane >= HEAD_DIM)
                acc[pair] = acc[pair] * jnp.where(here, factor, 1.0) + jnp.where(
                    here, part_sum, 0.0
                )

    kv[4 * PATCH : 8 * PATCH] = kv_now[...]
    attend(8 * PATCH, True, {1: functools.partial(near, 1), 4: far_first})

    def group(g):
        def when(table):
            def hook():
                for at, actions in table.items():
                    if g == at:
                        for action in actions:
                            action()
            return hook

        when({
            0: [arrival((1, 0), 1, None, 2), arrival((0, 1), 1, None, 2)],
            1: [arrival((1, 1), 1, None, 2), arrival((3, 1), 1, None, 2)],
            2: [arrival((2, 1), 1, None, 2), arrival((1, 2), 1, None, 2)],
        })()
        for dc in range(2):
            project(xall[g, dc], dc * 8 * PATCH)
        attend(16 * PATCH, False, {
            0: when({0: [far_second]}),
            2: when({0: [functools.partial(line, 1)], 1: [lines_far]}),
            3: when({0: [functools.partial(line, 3)], 1: [last_corner]}),
            4: when({0: [functools.partial(line, 2)]}),
        })

    for g in range(3):
        group(g)
    arrive((2, 0), 1)
    arrive((0, 2), 1)
    arrive((2, 2), 1)
    for dc in range(2):
        project(xall[3, dc, 1:4], dc * 6 * PATCH)

    r_copies = []

    def deliver(pairs):
        for pair in pairs:
            below = total[2 * pair]
            if pair < 2:
                below = jnp.where(lane < HEAD_DIM, below, total[2 * pair + 1])
            mixed = acc[pair] / below
            if pair == 2:
                mixed = jnp.where(lane // HEAD_DIM == core, mixed, 0.0)
            lanes = slice(128 * pair, 128 * pair + 128)
            result[:, :, :, lanes] = mixed.astype(BF16).reshape(4, 2, COLS, 128)
        lanes = pl.ds(128 * pairs[0], 128 * len(pairs))
        frame = 2 * part + y
        for flip, dc, dy in (
            (1, 1, 1), (1, 0, 1), (1, 1, 0), (1, 0, 0), (0, 1, 1), (0, 0, 1), (0, 1, 0)
        ):
            to_part = part + flip - 2 * part * flip
            at = len(r_copies)
            r_copies.append(remote(
                result.at[2 * dc + dy, to_part, :, lanes], mixes.at[frame, core, :, lanes],
                r_sent.at[at], r_recv.at[at], column(dc, dy, to_part),
            ))
            r_copies[-1].start()
        mixes[frame, core, :, lanes] = result[0, part, :, lanes]

    attend(12 * PATCH, False, {4: functools.partial(deliver, (0, 1))})
    deliver((2,))
    for copy in f_copies:
        copy.wait_recv()
    for copy in late_copies:
        copy.wait()
    for copy in r_copies:
        copy.wait_recv()

    rows = 4 * COLS
    middle = mixes[:, 0, :, 256:] + mixes[:, 1, :, 256:]
    mix = jnp.concatenate(
        [mixes[:, 0, :, :256], middle, mixes[:, 1, :, :256]], axis=-1
    ).reshape(rows, WIDTH)
    second = first_all[...].reshape(rows, WIDTH) + dot(mix, attn_out_w[...])
    third[...] = second
    time_qkv[...] = dot(layer_norm(second, gains_ref[1:2, :]), time_w[...]).astype(BF16)

    ones_row = lax.broadcasted_iota(jnp.int32, (256, 128), 0) % 128 // HEAD_DIM
    ones_col = lax.broadcasted_iota(jnp.int32, (256, 128), 1) // HEAD_DIM
    ones = jnp.where(ones_row == ones_col, 1.0, 0.0).astype(BF16)
    for pair in range(5):
        def lanes_of(kind):
            at = WIDTH * kind + 128 * pair
            return time_qkv[:, at : at + 128].reshape(4, COLS, 128).astype(F32)

        tq, tk, tv = lanes_of(0), lanes_of(1), lanes_of(2)
        products = (tq[:, None] * tk[None]).reshape(16 * COLS, 128)
        high = products.astype(BF16)
        low = (products - high.astype(F32)).astype(BF16)
        s = dot(jnp.concatenate([high, low], axis=1), ones) * lane_scale(1, pair)
        s = s.reshape(4, 4, COLS, 128)
        w = jnp.exp2(s - jnp.max(s, axis=1, keepdims=True))
        mixed = jnp.sum(w.astype(BF16).astype(F32) * tv[None], axis=1) / jnp.sum(w, axis=1)
        time_mix[:, 128 * pair : 128 * pair + 128] = mixed.astype(BF16).reshape(rows, 128)
    third[...] = third[...] + dot(time_mix[...], time_out_w[...])
    normed_three = layer_norm(third[...], gains_ref[2:3, :])
    for step in range(HIDDEN // FF_STEP):
        at = FF_STEP * step
        value = dot(normed_three, ff_in_w[:, at : at + FF_STEP])
        gate = dot(normed_three, ff_in_w[:, HIDDEN + at : HIDDEN + at + FF_STEP])
        gelu = 0.5 * gate * (1.0 + lax.erf(gate * math.sqrt(0.5)))
        hidden[:, at : at + FF_STEP] = (value * gelu).astype(BF16)
    half_rows = 2 * COLS
    mine = pl.ds(pl.multiple_of(part * half_rows, half_rows), half_rows)
    theirs = pl.ds(pl.multiple_of((1 - part) * half_rows, half_rows), half_rows)
    b_copies = []
    for at, count in ((0, 384), (384, 256)):
        lanes = slice(at, at + count)
        third[:, lanes] = third[:, lanes] + dot(hidden[...], ff_out_w[:, lanes])
        back[:, lanes] = third[theirs, lanes].astype(BF16)
        ref = pl.ds(at, count)
        b_copies.append(remote(
            back.at[:, ref], back_in.at[:, ref], b_sent.at[len(b_copies)],
            b_recv.at[len(b_copies)], partner,
        ))
        b_copies[-1].start()
    out_ref[:, part] = third[mine].reshape(2, COLS, WIDTH)
    for copy in b_copies:
        copy.wait_recv()
    out_ref[:, 1 - part] = back_in[...].astype(F32).reshape(2, COLS, WIDTH)
    for copy in started + r_copies + f_copies + b_copies + [norm_copy, lat_remote]:
        copy.wait_send()

    @pl.when(row > 0)
    def _():
        edges[0].wait_send()
        edges[1].wait_send()

    @pl.when(row < 63)
    def _():
        edges[2].wait_send()
        edges[3].wait_send()


def body(*arrays):
    vmem = pl.BlockSpec(memory_space=pltpu.VMEM)
    hbm = pl.BlockSpec(memory_space=pl.ANY)
    dma = pltpu.SemaphoreType.DMA
    rows = 4 * COLS
    return pl.pallas_call(
        block_kernel,
        out_shape=jax.ShapeDtypeStruct((2, 2, COLS, WIDTH), F32),
        in_specs=[hbm] * 3 + [vmem, pl.BlockSpec(memory_space=pltpu.SMEM)] + [hbm] * 7,
        out_specs=vmem,
        scratch_shapes=[
            pltpu.VMEM((2, 2, COLS, WIDTH), BF16),
            pltpu.VMEM((2, 2, COLS, WIDTH), BF16),
            pltpu.VMEM((2, 4, COLS, 3 * WIDTH), BF16),
            pltpu.VMEM((9, WIDTH, WIDTH), BF16),
            pltpu.VMEM((WIDTH, 3 * HALF), BF16),
            pltpu.VMEM((WIDTH, WIDTH), BF16),
            pltpu.VMEM((WIDTH, 3 * WIDTH), BF16),
            pltpu.VMEM((WIDTH, WIDTH), BF16),
            pltpu.VMEM((WIDTH, 2 * HIDDEN), BF16),
            pltpu.VMEM((HIDDEN, WIDTH), BF16),
            pltpu.VMEM((2, 2, COLS, WIDTH), F32),
            pltpu.VMEM((4, COLS, WIDTH), F32),
            pltpu.VMEM((2, 2, PATCH, WIDTH), BF16),
            pltpu.VMEM((QUERIES, 2 * HALF), BF16),
            pltpu.VMEM((4, 2, 4, 2, 2, COLS, WIDTH), BF16),
            pltpu.VMEM((5, QUERIES, 128), BF16),
            pltpu.VMEM((16 * PATCH, 2 * HALF), BF16),
            pltpu.VMEM((2, QUERIES, 16 * PATCH), F32),
            pltpu.VMEM((2, QUERIES, 128), F32),
            pltpu.VMEM((3, QUERIES, 128), F32),
            pltpu.VMEM((5, QUERIES, 128), F32),
            pltpu.VMEM((5, QUERIES, 128), F32),
            pltpu.VMEM((4, 2, COLS, HALF), BF16),
            pltpu.VMEM((4, 2, COLS, HALF), BF16),
            pltpu.VMEM((rows, 3 * WIDTH), BF16),
            pltpu.VMEM((rows, WIDTH), BF16),
            pltpu.VMEM((rows, WIDTH), F32),
            pltpu.VMEM((rows, HIDDEN), BF16),
            pltpu.VMEM((PATCH, WIDTH), BF16),
            pltpu.VMEM((PATCH, WIDTH), BF16),
            dma((15,)),
            dma((4, 2, 4, 2)),
            dma((48,)),
            dma((1,)),
            dma((1,)),
            dma((14,)),
            dma((14,)),
            dma((2, 2)),
            dma((2, 2)),
            dma((1,)),
            dma((1,)),
            dma((4,)),
            dma((4,)),
            dma((2,)),
            dma((2,)),
            dma((1,)),
        ],
        compiler_params=pltpu.CompilerParams(
            collective_id=0, has_side_effects=True, vmem_limit_bytes=62 << 20
        ),
        name="block",
    )(*arrays)


def solution(mesh):
    split = P("frames", "rows", None, None)
    return jax.shard_map(
        body,
        mesh=mesh,
        in_specs=(split,) * 3 + (P(),) * 9,
        out_specs=split,
        check_vma=False,
    )
```

```python
import functools
import math

import jax
import jax.numpy as jnp
from jax import lax
from jax.experimental import pallas as pl
from jax.experimental.pallas import tpu as pltpu
from jax.sharding import PartitionSpec as P

HEAD_DIM = 64
NEG = -1e30
EPS = 1e-05
F32 = jnp.float32
BF16 = jnp.bfloat16
MESH = pl.DeviceIdType.MESH
NT = (((1,), (1,)), ((), ()))
WIDTH = 640
COLS = 48
PATCH = 96
QUERIES = 384
HALF = 384
HIDDEN = 2560
FF_STEP = 512
LOG2E = math.log2(math.e)

SLOTS = {
    (1, 0): (0, 0), (3, 0): (0, 1), (0, 1): (0, 2), (0, 3): (0, 3),
    (1, 1): (1, 0), (1, 3): (1, 1), (3, 1): (1, 2), (3, 3): (1, 3),
    (2, 1): (2, 0), (2, 3): (2, 1), (1, 2): (2, 2), (3, 2): (2, 3),
    (0, 0): (3, 0), (2, 0): (3, 1), (0, 2): (3, 2), (2, 2): (3, 3),
}


def dot(left, right):
    return jnp.dot(left, right, preferred_element_type=F32)


def layer_norm(values, gain):
    centre = values - jnp.mean(values, axis=-1, keepdims=True)
    spread = jnp.mean(centre * centre, axis=-1, keepdims=True)
    return (centre * lax.rsqrt(spread + EPS) * gain).astype(BF16)


def block_kernel(
    latents_hbm, previous_hbm, stale_hbm, gains_ref, scale_ref, conv_hbm, attn_hbm, attn_out_hbm,
    time_hbm, time_out_hbm, ff_in_hbm, ff_out_hbm,
    out_ref,
    lat, halo, field, conv_w, wall, attn_out_w, time_w, time_out_w, ff_in_w, ff_out_w,
    first, first_all, norm_in, kv_now, xall, q_heads, kv, scores, top, acc, peak, total,
    result, mixes, time_qkv, time_mix, third, hidden, back, back_in,
    load, recv, sent, n_recv, n_sent, r_recv, r_sent, h_recv, h_sent, l_recv, l_sent,
    f_recv, f_sent, b_recv, b_sent, local,
):
    row = lax.axis_index("rows")
    part = lax.axis_index("frames")
    core = row % 2
    z = (row // 2) % 4
    y = (row // 8) % 2
    x = row // 16

    def device(x, y, z, core, part=part):
        return (((x * 2 + y) * 4 + z) * 2 + core, part)

    def ring(along_first, step):
        dx = step * (1 - core) if along_first else step * core
        dz = step * core if along_first else step * (1 - core)
        return device((x + dx + 4) % 4, y, (z + dz + 4) % 4, core)

    a_up, a_down = ring(True, 1), ring(True, -1)
    b_up, b_down = ring(False, 1), ring(False, -1)

    def column(dc, dy, part):
        return device(x, (y + dy) % 2, z, (core + dc) % 2, part)

    mate, across = column(1, 0, part), column(0, 1, part)
    quad = [(0, 1, across), (1, 0, mate), (1, 1, column(1, 1, part))]
    partner = (row, 1 - part)
    patches = (row, row + 8 - 16 * y)

    loads = []

    def fetch(src, dst):
        copy = pltpu.make_async_copy(src, dst, load.at[len(loads)])
        loads.append(copy)
        copy.start()
        return copy

    lat_copy = fetch(latents_hbm.at[y], lat.at[0])
    conv_copies = [
        fetch(conv_hbm.at[pl.ds(3 * tap, 3)], conv_w.at[pl.ds(3 * tap, 3)]) for tap in (1, 0, 2)
    ]

    barrier = pltpu.get_barrier_semaphore()

    def greet(other):
        pl.semaphore_signal(barrier, inc=1, device_id=other, device_id_type=MESH)

    for other in (a_up, a_down, b_up, b_down) + tuple(item[2] for item in quad):
        greet(other)
    for dc in range(2):
        for dy in range(2):
            greet(column(dc, dy, 1 - part))

    for patch in patches:
        @pl.when(patch > 0)
        def _():
            greet((patch - 1, part))

        @pl.when(patch < 63)
        def _():
            greet((patch + 1, part))

    wall_copies = []
    for kind in range(3):
        wall_copies.append(fetch(
            attn_hbm.at[:, pl.ds(pl.multiple_of(WIDTH * kind + 384 * core, 128), 256)],
            wall.at[:, pl.ds(HALF * kind, 256)],
        ))
        wall_copies.append(fetch(
            attn_hbm.at[:, pl.ds(WIDTH * kind + 256, 128)],
            wall.at[:, pl.ds(HALF * kind + 256, 128)],
        ))
    late_copies = [
        fetch(attn_out_hbm, attn_out_w), fetch(time_hbm, time_w), fetch(time_out_hbm, time_out_w),
        fetch(ff_in_hbm, ff_in_w), fetch(ff_out_hbm, ff_out_w),
    ]

    @pl.when((row > 0) & (row < 63))
    def _():
        pl.semaphore_wait(barrier, 15)

    @pl.when((row == 0) | (row == 63))
    def _():
        pl.semaphore_wait(barrier, 13)

    started = []

    def remote(src, dst, send_sem, recv_sem, to):
        return pltpu.make_async_remote_copy(
            src_ref=src, dst_ref=dst, send_sem=send_sem, recv_sem=recv_sem,
            device_id=to, device_id_type=MESH,
        )

    lat_remote = remote(latents_hbm.at[1 - y], lat.at[1], l_sent.at[0], l_recv.at[0], across)
    lat_remote.start()
    edges = []
    for side in range(2):
        patch = row - 1 + 2 * side
        for frame in range(2):
            to = device(patch // 16, frame, (patch // 2) % 4, patch % 2)
            dy = ((patch // 8) % 2 + frame) % 2
            edges.append(remote(
                previous_hbm.at[frame, side], halo.at[dy, 1 - side],
                h_sent.at[side, frame], h_recv.at[dy, 1 - side], to,
            ))

    @pl.when(row > 0)
    def _():
        edges[0].start()
        edges[1].start()

    @pl.when(row < 63)
    def _():
        edges[2].start()
        edges[3].start()

    def send(src, at, to, dc=0, dy=None, places=1):
        group, place = SLOTS[at]
        if dy is not None:
            dst = xall.at[group, dc, place, dy]
        else:
            dst = xall.at[group, dc, pl.ds(place, places)]
        copy = remote(
            src, dst, sent.at[len(started)], recv.at[group, dc, place, dy or 0], to
        )
        started.append(copy)
        return copy

    def arrival(at, dc=0, dy=None, places=1):
        group, place = SLOTS[at]
        if dy is not None:
            dst = xall.at[group, dc, place, dy]
        else:
            dst = xall.at[group, dc, pl.ds(place, places)]
        sem = recv.at[group, dc, place, dy or 0]
        return lambda: remote(dst, dst, sem, sem, mate).wait_recv()

    def held(at, dy=None, places=1):
        group, place = SLOTS[at]
        if dy is not None:
            return xall.at[group, 0, place, dy]
        return xall.at[group, 0, pl.ds(place, places)]

    def arrive(at, dc=0, dy=None, places=1):
        arrival(at, dc, dy, places)()

    def own_ways(src, dy):
        return [
            send(src, (3, 0), a_up, dy=dy), send(src, (1, 0), a_down, dy=dy),
            send(src, (0, 3), b_up, dy=dy), send(src, (0, 1), b_down, dy=dy),
            send(src, (0, 0), mate, dc=1, dy=dy),
        ]

    def start(copies):
        for copy in copies:
            copy.start()

    own = stale_hbm.at[y]
    start([send(stale_hbm.at[1 - y], (0, 0), across, dy=1)])
    start(own_ways(own, 0))
    keep_own = pltpu.make_async_copy(own, held((0, 0), 0), local.at[0])
    keep_own.start()

    near_a = [
        [send(held((3, 0), 0), (2, 0), a_up, dy=0)], [send(held((1, 0), 1), (2, 0), a_down, dy=1)]
    ]
    near_b = [
        [send(held((0, 3), 0), (0, 2), b_up, dy=0)], [send(held((0, 1), 1), (0, 2), b_down, dy=1)]
    ]
    lines_b = {
        (da, dy): [
            send(held((da, 0), dy), (da, 3), b_up, dy=dy),
            send(held((da, 0), dy), (da, 1), b_down, dy=dy),
        ]
        for da in (1, 3, 2) for dy in range(2)
    }
    ahead = {
        da: [
            send(held((da, 3), 0), (da, 2), b_up, dy=0),
            send(held((da, 1), 1), (da, 2), b_down, dy=1),
        ]
        for da in (1, 3, 2)
    }
    to_mate = {
        at: [send(held(at, places=count), at, mate, dc=1, places=count)]
        for at, count in (
            ((1, 0), 2), ((0, 1), 2), ((1, 1), 2), ((3, 1), 2), ((2, 1), 2), ((1, 2), 2),
            ((2, 0), 1), ((0, 2), 1), ((2, 2), 1),
        )
    }
    dy_ways = own_ways(held((0, 0), 1), 1)

    def own_second():
        arrive((0, 0), dy=1)
        start(dy_ways)

    def near(dy):
        for da in (3, 1):
            arrive((da, 0), dy=dy)
        start(near_a[dy])
        for da in (1, 3):
            start(lines_b[da, dy])
        for db in (3, 1):
            arrive((0, db), dy=dy)
        start(near_b[dy])
        if dy == 1:
            start(to_mate[1, 0])
            start(to_mate[0, 1])

    def far_first():
        for dy in range(2):
            arrive((2, 0), dy=dy)
            start(lines_b[2, dy])
        start(to_mate[2, 0])

    def far_second():
        for dy in range(2):
            arrive((0, 2), dy=dy)
        start(to_mate[0, 2])

    def line(da):
        arrive((da, 3), dy=0)
        arrive((da, 1), dy=1)
        start(ahead[da])
        arrive((da, 3), dy=1)
        arrive((da, 1), dy=0)
        start(to_mate[da, 1])

    def lines_far():
        for da in (1, 3):
            for dy in range(2):
                arrive((da, 2), dy=dy)
        start(to_mate[1, 2])

    def last_corner():
        for dy in range(2):
            arrive((2, 2), dy=dy)
        start(to_mate[2, 2])

    column_at = lax.broadcasted_iota(jnp.int32, (COLS, WIDTH), 0)

    def fill(dy, at, values):
        cells = values.astype(F32)
        cells = cells * (1.0 / (1.0 + jnp.exp(-cells)))
        left = jnp.where(column_at == 0, 0.0, pltpu.roll(cells, 1, 0))
        right = jnp.where(column_at == COLS - 1, 0.0, pltpu.roll(cells, COLS - 1, 0))
        field[dy, at, :, :WIDTH] = left.astype(BF16)
        field[dy, at, :, WIDTH : 2 * WIDTH] = cells.astype(BF16)
        field[dy, at, :, 2 * WIDTH :] = right.astype(BF16)

    def taps(at):
        return dot(
            field[:, at : at + 2].reshape(2 * PATCH, 3 * WIDTH),
            conv_w[3 * at : 3 * at + 3].reshape(3 * WIDTH, WIDTH),
        )

    lat_copy.wait()
    fill(0, 1, lat[0, 0])
    fill(0, 2, lat[0, 1])
    for dy in range(2):
        for side in range(2):
            there = patches[dy] > 0 if side == 0 else patches[dy] < 63
            gone = patches[dy] == 0 if side == 0 else patches[dy] == 63
            edge = halo.at[dy, side]
            sem = h_recv.at[dy, side]

            @pl.when(there)
            def _():
                remote(edge, edge, sem, sem, mate).wait_recv()

            @pl.when(gone)
            def _():
                halo[dy, side] = jnp.zeros_like(halo[dy, side])

            fill(dy, 3 * side, halo[dy, side])
    lat_remote.wait_recv()
    fill(1, 1, lat[1, 0])
    fill(1, 2, lat[1, 1])
    near(0)
    own_second()
    conv_copies[0].wait()
    conv_sum = taps(1)
    conv_copies[1].wait()
    conv_sum = conv_sum + taps(0)
    conv_copies[2].wait()
    conv_sum = conv_sum + taps(2)
    start_sum = lat[...].reshape(2 * PATCH, WIDTH).astype(F32) + conv_sum
    norm_in[0] = layer_norm(start_sum, gains_ref[0:1, :]).reshape(2, PATCH, WIDTH)
    norm_copy = remote(norm_in.at[0], norm_in.at[1], n_sent.at[0], n_recv.at[0], mate)
    norm_copy.start()
    first[...] = start_sum.reshape(2, 2, COLS, WIDTH)
    frame_here = 2 * part + y
    f_copies = []
    for dy, flip in ((0, 1), (1, 0), (1, 1)):
        to_part = part + flip - 2 * part * flip
        at = 2 * dy + flip
        f_copies.append(remote(
            first.at[dy, to_part], first_all.at[frame_here], f_sent.at[at], f_recv.at[at],
            column(0, dy, to_part),
        ))
    start(f_copies)
    first_all[frame_here] = first[0, part]
    for copy in wall_copies:
        copy.wait()
    lane = lax.broadcasted_iota(jnp.int32, (QUERIES, 128), 1)
    half_lane = lax.broadcasted_iota(jnp.int32, (1, 128), 1) // HEAD_DIM

    def lane_scale(kind, pair):
        low, high = scale_ref[kind, 2 * pair], scale_ref[kind, 2 * pair + 1]
        return jnp.where(half_lane == 0, low, high) * (LOG2E / math.sqrt(HEAD_DIM))

    def project(rows, at):
        count = rows.shape[0] * rows.shape[1] * rows.shape[2] * rows.shape[3]
        kv[at : at + count] = dot(rows.reshape(count, WIDTH), wall[:, HALF:]).astype(BF16)

    keep_own.wait()
    arrive((0, 0), dc=1, dy=0)
    arrive((0, 0), dc=1, dy=1)
    for dc in range(2):
        project(xall[3, dc, 0:1], dc * 2 * PATCH)

    norm_copy.wait_recv()
    triple = dot(norm_in[...].reshape(QUERIES, WIDTH), wall[...])
    kv_now[...] = triple[:, HALF:].astype(BF16)
    for place, pair in enumerate((3 * core, 3 * core + 1, 2)):
        both = triple[:, 128 * place : 128 * place + 128] * lane_scale(0, pair)
        both = both.astype(BF16)
        zero = jnp.zeros_like(both)
        if place < 2:
            q_heads[2 * place] = jnp.where(lane < HEAD_DIM, both, zero)
            q_heads[2 * place + 1] = jnp.where(lane < HEAD_DIM, zero, both)
        else:
            q_heads[4] = jnp.where(lane // HEAD_DIM == core, both, zero)
    acc[...] = jnp.zeros_like(acc)
    total[...] = jnp.zeros_like(total)
    peak[...] = jnp.full_like(peak, NEG)

    def attend(keys, masked, hooks):
        def keys_of(head):
            at = 128 * (head // 2)
            return kv[:keys, at : at + 128]

        def score(head):
            s = lax.dot_general(q_heads[head], keys_of(head), NT, preferred_element_type=F32)
            if masked:
                q_patch = lax.broadcasted_iota(jnp.int32, (QUERIES, keys), 0) // PATCH
                k_patch = lax.broadcasted_iota(jnp.int32, (QUERIES, keys), 1) // PATCH
                drop = ((k_patch < 4) & (k_patch == q_patch)) | (
                    (k_patch >= 4) & (k_patch != q_patch + 4)
                )
                s = jnp.where(drop, NEG, s)
            scores[head % 2, :, :keys] = s
            top[head % 2] = jnp.broadcast_to(jnp.max(s, axis=1, keepdims=True), (QUERIES, 128))

        score(0)
        for head in range(5):
            if head in hooks:
                hooks[head]()
            if head < 4:
                score(head + 1)
            pair = head // 2
            old = peak[head]
            new = jnp.maximum(old, top[head % 2])
            factor = jnp.exp2(old - new)
            peak[head] = new
            w = jnp.exp2(scores[head % 2, :, :keys] - new[:, :1])
            total[head] = total[head] * factor + jnp.sum(w, axis=1, keepdims=True)
            at = HALF + 128 * pair
            part_sum = dot(w.astype(BF16), kv[:keys, at : at + 128])
            if head == 4:
                acc[pair] = acc[pair] * factor + part_sum
            else:
                here = (lane < HEAD_DIM) if head % 2 == 0 else (lane >= HEAD_DIM)
                acc[pair] = acc[pair] * jnp.where(here, factor, 1.0) + jnp.where(
                    here, part_sum, 0.0
                )

    kv[4 * PATCH : 8 * PATCH] = kv_now[...]
    attend(8 * PATCH, True, {1: functools.partial(near, 1), 4: far_first})

    def group(g):
        def when(table):
            def hook():
                for at, actions in table.items():
                    if g == at:
                        for action in actions:
                            action()
            return hook

        project(xall[g, 0], 0)
        when({
            0: [arrival((1, 0), 1, None, 2), arrival((0, 1), 1, None, 2)],
            1: [arrival((1, 1), 1, None, 2), arrival((3, 1), 1, None, 2)],
            2: [arrival((2, 1), 1, None, 2), arrival((1, 2), 1, None, 2)],
        })()
        project(xall[g, 1], 8 * PATCH)
        attend(16 * PATCH, False, {
            0: when({0: [far_second]}),
            2: when({0: [functools.partial(line, 1)], 1: [lines_far]}),
            3: when({0: [functools.partial(line, 3)], 1: [last_corner]}),
            4: when({0: [functools.partial(line, 2)]}),
        })

    for g in range(3):
        group(g)
    project(xall[3, 0, 1:4], 0)
    arrive((2, 0), 1)
    arrive((0, 2), 1)
    arrive((2, 2), 1)
    project(xall[3, 1, 1:4], 6 * PATCH)

    r_copies = []

    def deliver(pairs):
        for pair in pairs:
            below = total[2 * pair]
            if pair < 2:
                below = jnp.where(lane < HEAD_DIM, below, total[2 * pair + 1])
            mixed = acc[pair] / below
            if pair == 2:
                mixed = jnp.where(lane // HEAD_DIM == core, mixed, 0.0)
            lanes = slice(128 * pair, 128 * pair + 128)
            result[:, :, :, lanes] = mixed.astype(BF16).reshape(4, 2, COLS, 128)
        lanes = pl.ds(128 * pairs[0], 128 * len(pairs))
        frame = 2 * part + y
        for flip, dc, dy in (
            (1, 1, 1), (1, 0, 1), (1, 1, 0), (1, 0, 0), (0, 1, 1), (0, 0, 1), (0, 1, 0)
        ):
            to_part = part + flip - 2 * part * flip
            at = len(r_copies)
            r_copies.append(remote(
                result.at[2 * dc + dy, to_part, :, lanes], mixes.at[frame, core, :, lanes],
                r_sent.at[at], r_recv.at[at], column(dc, dy, to_part),
            ))
            r_copies[-1].start()
        mixes[frame, core, :, lanes] = result[0, part, :, lanes]

    attend(12 * PATCH, False, {
        2: functools.partial(deliver, (0,)), 4: functools.partial(deliver, (1,)),
    })
    deliver((2,))
    for copy in f_copies:
        copy.wait_recv()
    for copy in late_copies:
        copy.wait()
    for copy in r_copies:
        copy.wait_recv()

    rows = 4 * COLS
    middle = mixes[:, 0, :, 256:] + mixes[:, 1, :, 256:]
    mix = jnp.concatenate(
        [mixes[:, 0, :, :256], middle, mixes[:, 1, :, :256]], axis=-1
    ).reshape(rows, WIDTH)
    second = first_all[...].reshape(rows, WIDTH) + dot(mix, attn_out_w[...])
    third[...] = second
    time_qkv[...] = dot(layer_norm(second, gains_ref[1:2, :]), time_w[...]).astype(BF16)

    ones_row = lax.broadcasted_iota(jnp.int32, (256, 128), 0) % 128 // HEAD_DIM
    ones_col = lax.broadcasted_iota(jnp.int32, (256, 128), 1) // HEAD_DIM
    ones = jnp.where(ones_row == ones_col, 1.0, 0.0).astype(BF16)
    for pair in range(5):
        def lanes_of(kind):
            at = WIDTH * kind + 128 * pair
            return time_qkv[:, at : at + 128].reshape(4, COLS, 128).astype(F32)

        tq, tk, tv = lanes_of(0), lanes_of(1), lanes_of(2)
        products = (tq[:, None] * tk[None]).reshape(16 * COLS, 128)
        high = products.astype(BF16)
        low = (products - high.astype(F32)).astype(BF16)
        s = dot(jnp.concatenate([high, low], axis=1), ones) * lane_scale(1, pair)
        s = s.reshape(4, 4, COLS, 128)
        w = jnp.exp2(s - jnp.max(s, axis=1, keepdims=True))
        mixed = jnp.sum(w.astype(BF16).astype(F32) * tv[None], axis=1) / jnp.sum(w, axis=1)
        time_mix[:, 128 * pair : 128 * pair + 128] = mixed.astype(BF16).reshape(rows, 128)
    third[...] = third[...] + dot(time_mix[...], time_out_w[...])
    normed_three = layer_norm(third[...], gains_ref[2:3, :])
    for step in range(HIDDEN // FF_STEP):
        at = FF_STEP * step
        value = dot(normed_three, ff_in_w[:, at : at + FF_STEP])
        gate = dot(normed_three, ff_in_w[:, HIDDEN + at : HIDDEN + at + FF_STEP])
        gelu = 0.5 * gate * (1.0 + lax.erf(gate * math.sqrt(0.5)))
        hidden[:, at : at + FF_STEP] = (value * gelu).astype(BF16)
    half_rows = 2 * COLS
    mine = pl.ds(pl.multiple_of(part * half_rows, half_rows), half_rows)
    theirs = pl.ds(pl.multiple_of((1 - part) * half_rows, half_rows), half_rows)
    b_copies = []
    for at, count in ((0, 384), (384, 256)):
        lanes = slice(at, at + count)
        third[:, lanes] = third[:, lanes] + dot(hidden[...], ff_out_w[:, lanes])
        back[:, lanes] = third[theirs, lanes].astype(BF16)
        ref = pl.ds(at, count)
        b_copies.append(remote(
            back.at[:, ref], back_in.at[:, ref], b_sent.at[len(b_copies)],
            b_recv.at[len(b_copies)], partner,
        ))
        b_copies[-1].start()
    out_ref[:, part] = third[mine].reshape(2, COLS, WIDTH)
    for copy in b_copies:
        copy.wait_recv()
    out_ref[:, 1 - part] = back_in[...].astype(F32).reshape(2, COLS, WIDTH)
    for copy in started + r_copies + f_copies + b_copies + [norm_copy, lat_remote]:
        copy.wait_send()

    @pl.when(row > 0)
    def _():
        edges[0].wait_send()
        edges[1].wait_send()

    @pl.when(row < 63)
    def _():
        edges[2].wait_send()
        edges[3].wait_send()


def body(*arrays):
    vmem = pl.BlockSpec(memory_space=pltpu.VMEM)
    hbm = pl.BlockSpec(memory_space=pl.ANY)
    dma = pltpu.SemaphoreType.DMA
    rows = 4 * COLS
    return pl.pallas_call(
        block_kernel,
        out_shape=jax.ShapeDtypeStruct((2, 2, COLS, WIDTH), F32),
        in_specs=[hbm] * 3 + [vmem, pl.BlockSpec(memory_space=pltpu.SMEM)] + [hbm] * 7,
        out_specs=vmem,
        scratch_shapes=[
            pltpu.VMEM((2, 2, COLS, WIDTH), BF16),
            pltpu.VMEM((2, 2, COLS, WIDTH), BF16),
            pltpu.VMEM((2, 4, COLS, 3 * WIDTH), BF16),
            pltpu.VMEM((9, WIDTH, WIDTH), BF16),
            pltpu.VMEM((WIDTH, 3 * HALF), BF16),
            pltpu.VMEM((WIDTH, WIDTH), BF16),
            pltpu.VMEM((WIDTH, 3 * WIDTH), BF16),
            pltpu.VMEM((WIDTH, WIDTH), BF16),
            pltpu.VMEM((WIDTH, 2 * HIDDEN), BF16),
            pltpu.VMEM((HIDDEN, WIDTH), BF16),
            pltpu.VMEM((2, 2, COLS, WIDTH), F32),
            pltpu.VMEM((4, COLS, WIDTH), F32),
            pltpu.VMEM((2, 2, PATCH, WIDTH), BF16),
            pltpu.VMEM((QUERIES, 2 * HALF), BF16),
            pltpu.VMEM((4, 2, 4, 2, 2, COLS, WIDTH), BF16),
            pltpu.VMEM((5, QUERIES, 128), BF16),
            pltpu.VMEM((16 * PATCH, 2 * HALF), BF16),
            pltpu.VMEM((2, QUERIES, 16 * PATCH), F32),
            pltpu.VMEM((2, QUERIES, 128), F32),
            pltpu.VMEM((3, QUERIES, 128), F32),
            pltpu.VMEM((5, QUERIES, 128), F32),
            pltpu.VMEM((5, QUERIES, 128), F32),
            pltpu.VMEM((4, 2, COLS, HALF), BF16),
            pltpu.VMEM((4, 2, COLS, HALF), BF16),
            pltpu.VMEM((rows, 3 * WIDTH), BF16),
            pltpu.VMEM((rows, WIDTH), BF16),
            pltpu.VMEM((rows, WIDTH), F32),
            pltpu.VMEM((rows, HIDDEN), BF16),
            pltpu.VMEM((PATCH, WIDTH), BF16),
            pltpu.VMEM((PATCH, WIDTH), BF16),
            dma((15,)),
            dma((4, 2, 4, 2)),
            dma((48,)),
            dma((1,)),
            dma((1,)),
            dma((21,)),
            dma((21,)),
            dma((2, 2)),
            dma((2, 2)),
            dma((1,)),
            dma((1,)),
            dma((4,)),
            dma((4,)),
            dma((2,)),
            dma((2,)),
            dma((1,)),
        ],
        compiler_params=pltpu.CompilerParams(
            collective_id=0, has_side_effects=True, vmem_limit_bytes=62 << 20
        ),
        name="block",
    )(*arrays)


def solution(mesh):
    split = P("frames", "rows", None, None)
    return jax.shard_map(
        body,
        mesh=mesh,
        in_specs=(split,) * 3 + (P(),) * 9,
        out_specs=split,
        check_vma=False,
    )
```
